32 devices in a mesh: space: 4 (over x, core), term: 8 (over z, y).
Axes of the slice: x: 2, y: 2, z: 4, core: 2. Of those that a mesh axis runs over, the one named last changes fastest.
Arguments:
- right_modes: float32 [32, 64, 256], P(('space', 'term')), may hold values from -0.0625 to 0.0625
- adjoint_modes: float32 [32, 64, 256], P(('space', 'term')), may hold values from -6 to 6
- conductivity_terms: float32 [32, 256, 256], P('space', 'term'), may hold values from -6 to 6
Outputs:
- reduced_blocks: float32 [256, 4096], P('term', 'space')
The draws below stay inside these ranges and needn't reach their ends.
All inputs are finite; a program needn't handle non-finite values.
Results may differ from the reference program's by a relative error of at most 0.000098.
Values sent between devices are 32-bit elements; how exact they have to be, the bound alone decides.
No kernel may reach another device: no remote copies, remote signals or barrier semaphores. Data moves between devices by JAX's collectives and lax.ppermute only.
A program may use at most 64 MiB of HBM per device.

```python
import jax
import jax.numpy as jnp
from jax import lax

R = 64
Q = 256
GX = 8
GY = 32
NZ = 32
PLANE = 256


def steps_of(rng, extent, pieces, low, high):
    factor_of = 1.0
    for axis_at, blocks in pieces:
        heights = jax.random.uniform(jax.random.fold_in(jax.random.fold_in(rng, 6), axis_at), (blocks,), jnp.float32, low / len(pieces), high / len(pieces))
        factor_of = factor_of * jnp.repeat(jnp.exp(heights), extent[axis_at] // blocks).reshape((-1,) + (1,) * (len(extent) - 1 - axis_at))
    return factor_of


def noise(own_key, extent, scale, most, pieces=(), dtype=jnp.bfloat16):
    entries = scale * jax.random.normal(own_key, extent, jnp.float32)
    if pieces:
        entries = entries * steps_of(own_key, extent, pieces, -0.22, 0.18)
    return jnp.clip(entries, -most, most).astype(dtype)


def setup_inputs(seed: int = 0) -> dict:
    key_of = jax.random.split(jax.random.key(seed), 4)
    return {
        "right_modes": noise(key_of[0], (NZ, R, PLANE), (NZ * GX * GY) ** -0.5, 0.0625, ((0, 32),), jnp.float32),
        "adjoint_modes": noise(key_of[1], (NZ, R, PLANE), 1.0, 6.0, ((0, 32),), jnp.float32),
        "conductivity_terms": noise(key_of[2], (NZ, Q, PLANE), 1.0, 6.0, ((0, 4), (1, 8)), jnp.float32),
    }


def shifted_cells(values, offset):
    zeros = jnp.zeros(values.shape[:-1] + (abs(offset),), jnp.float32)
    if offset > 0:
        return jnp.concatenate([values[..., offset:], zeros], axis=-1)
    return jnp.concatenate([zeros, values[..., :offset]], axis=-1)


def apply_terms(field_pad, coeff_pad, row_len):
    width = field_pad.shape[-1]
    column = jnp.arange(width) % row_len
    keep_next = (column != row_len - 1).astype(jnp.float32)
    keep_prev = (column != 0).astype(jnp.float32)
    centre = field_pad[None, 1:-1]
    coeff = coeff_pad[:, 1:-1, None, :]
    pairs = [
        (field_pad[None, 2:], coeff_pad[:, 2:, None, :]),
        (field_pad[None, :-2], coeff_pad[:, :-2, None, :]),
        (shifted_cells(centre, row_len), shifted_cells(coeff, row_len)),
        (shifted_cells(centre, -row_len), shifted_cells(coeff, -row_len)),
        (shifted_cells(centre, 1) * keep_next, shifted_cells(coeff, 1) * keep_next),
        (shifted_cells(centre, -1) * keep_prev, shifted_cells(coeff, -1) * keep_prev),
    ]
    result = jnp.zeros(coeff.shape[:2] + centre.shape[2:], jnp.float32)
    for other_field, other_coeff in pairs:
        result = result + 0.5 * (coeff + other_coeff) * (centre - other_field)
    return result


def project(adjoint, image):
    return jnp.einsum("zrp,gzsp->grs", adjoint, image, precision=lax.Precision.HIGHEST)


def reference(right_modes, adjoint_modes, conductivity_terms):
    field_pad = jnp.pad(right_modes, ((1, 1), (0, 0), (0, 0)))
    coeff_pad = jnp.moveaxis(jnp.pad(conductivity_terms, ((1, 1), (0, 0), (0, 0))), 1, 0)

    def one_term(coeff):
        image = apply_terms(field_pad, coeff[None], GY)
        return project(adjoint_modes, image)[0]

    blocks = lax.map(one_term, coeff_pad)
    return blocks.reshape(Q, R * R)
```

```python
import functools

import jax
import jax.numpy as jnp
from jax import lax
from jax.experimental import pallas as pl
from jax.experimental.pallas import tpu as pltpu
from jax.sharding import PartitionSpec as P

GY = 32
OFFSETS = (GY, -GY, 1, -1)
NT = (((1,), (1,)), ((), ()))
F32 = jnp.float32
BF16 = jnp.bfloat16


def shifted(values, offset):
    width = values.shape[-1]
    lane = lax.broadcasted_iota(jnp.int32, values.shape, values.ndim - 1)
    moved = pltpu.roll(values, (-offset) % width, values.ndim - 1)
    if offset == GY:
        keep = lane < width - GY
    elif offset == -GY:
        keep = lane >= GY
    elif offset == 1:
        keep = lane % GY != GY - 1
    else:
        keep = lane % GY != 0
    return jnp.where(keep, moved, 0.0)


def split(values):
    high = values.astype(BF16)
    return high, (values - high.astype(F32)).astype(BF16)


def stage_kernel(stage, first, last, n_term, n_space, chunk, *refs):
    k_ref = refs[0]
    blocks = refs[1 : 3 + 2 * stage]
    rest = list(refs[3 + 2 * stage :])
    pairs = n_term // 2
    far = stage >= pairs // 2
    halo_ref = rest.pop(0) if far else None
    before_ref = None if first else rest.pop(0)
    if last:
        keep_ref, send_ref, acc_ref = rest[:3]
        rest = rest[3:]
    else:
        acc_ref = rest.pop(0)
    da_ref, kb_ref, w_ref, wz_ref = rest
    modes = blocks[0].shape[1]
    terms = k_ref.shape[1]
    cells = k_ref.shape[2]
    term_at = lax.axis_index("term")
    space_at = lax.axis_index("space")
    z, y = term_at // 2, term_at % 2
    w = z ^ stage
    own_ref, other_ref = blocks[2 * stage], blocks[2 * stage + 1]

    coeffs = (k_ref[2 * w + y], k_ref[2 * w + 1 - y])
    for m, ref in enumerate((own_ref, other_ref)):
        a = ref[1]
        for d, offset in enumerate(OFFSETS):
            da_ref[4 * m + d] = a - shifted(a, offset)
            kb_ref[4 * m + d] = 0.5 * (coeffs[m] + shifted(coeffs[m], offset))
        high, low = split(ref[0])
        both = jnp.concatenate([high, low], 0)
        w_ref[:, 2 * m * cells : (2 * m + 1) * cells] = both
        w_ref[:, (2 * m + 1) * cells : (2 * m + 2) * cells] = both
    da_ref[8] = own_ref[1] - other_ref[1]
    kb_ref[8] = 0.5 * (coeffs[0] + coeffs[1])

    def body(c, carry):
        rows_a, rows_b = [], []
        for step in range(chunk):
            def term_of(d):
                return kb_ref[d] * da_ref[d, pl.ds(c * chunk + step, 1), :]

            across = term_of(8)
            rows_a.append(term_of(0) + term_of(1) + term_of(2) + term_of(3) + across)
            rows_b.append(term_of(4) + term_of(5) + term_of(6) + term_of(7) - across)
        left = jnp.concatenate(
            split(jnp.concatenate(rows_a, 0)) + split(jnp.concatenate(rows_b, 0)), 1
        )
        out = lax.dot_general(left, w_ref[...], NT, preferred_element_type=F32)
        out = out.reshape(chunk, terms, 2 * modes)
        at = pl.ds(c * chunk, chunk)
        acc_ref[at] = out if first else before_ref[at] + out
        return carry

    lax.fori_loop(0, modes // chunk, body, 0)

    def layer():
        def layer_body(c, carry):
            rows = [
                kb_ref[8] * da_ref[8, pl.ds(c * chunk + step, 1), :] for step in range(chunk)
            ]
            left = jnp.concatenate(split(jnp.concatenate(rows, 0)), 1)
            out = lax.dot_general(left, wz_ref[...], NT, preferred_element_type=F32)
            acc_ref[pl.ds(c * chunk, chunk)] += out.reshape(chunk, terms, 2 * modes)
            return carry

        lax.fori_loop(0, modes // chunk, layer_body, 0)

    def edge(first_side, second_side, coeff):
        da_ref[8] = first_side[1] - second_side[1]
        kb_ref[8] = coeff
        high, low = split(first_side[0] - second_side[0])
        both = jnp.concatenate([high, low], 0)
        wz_ref[:, :cells] = both
        wz_ref[:, cells:] = both

    for upward in (0, 1):
        near_w = w + 1 if upward else w - 1
        for j in range(stage):
            for parity in (0, 1):
                @pl.when((near_w >= 0) & (near_w < pairs) & (near_w ^ z == j) & (y == parity))
                def _():
                    here = own_ref if parity == upward else other_ref
                    there = blocks[2 * j] if parity == 1 - upward else blocks[2 * j + 1]
                    plane = 2 * w + upward
                    edge(
                        here,
                        there,
                        0.5 * (k_ref[plane] + k_ref[plane + (1 if upward else -1)]),
                    )

        if stage:
            @pl.when((near_w >= 0) & (near_w < pairs) & (near_w ^ z < stage))
            def _():
                layer()

    is_low = term_at < n_term // 2
    for upward in (0, 1):
        at_rim = w == (pairs - 1 if upward else 0)
        plane = n_term - 1 if upward else 0
        near_side = jnp.logical_not(is_low) if upward else is_low
        if far:
            used = at_rim & jnp.logical_not(near_side)
        else:
            used = at_rim & near_side & (space_at == (n_space - 1 if upward else 0))
        for parity in (0, 1):
            @pl.when(used & (y == parity))
            def _():
                here = own_ref if parity == upward else other_ref
                if far:
                    halo = (halo_ref[:modes], halo_ref[modes : 2 * modes])
                    edge(here, halo, 0.5 * (k_ref[plane] + halo_ref[2 * modes :]))
                else:
                    edge(here, (0.0, 0.0), 0.5 * k_ref[plane])

        @pl.when(used)
        def _():
            layer()

    if last:
        core = space_at % 2
        rows = modes // n_space
        lane = lax.broadcasted_iota(jnp.int32, (terms, 2 * modes), 1)

        def pack(block, out_ref, index):
            for j in range(rows // 2):
                even = acc_ref[block * rows + 2 * j]
                odd = acc_ref[block * rows + 2 * j + 1]
                even = even + pltpu.roll(even, modes, 1)
                odd = odd + pltpu.roll(odd, modes, 1)
                out_ref[index, j] = jnp.where(lane < modes, even, odd)

        def pack_body(index, carry):
            pack(2 * index + core, keep_ref, index)
            pack(2 * index + 1 - core, send_ref, index)
            return carry

        lax.fori_loop(0, n_space // 2, pack_body, 0)


def run_stage(stage, n_term, n_space, coeffs, blocks, halo, before):
    pairs = n_term // 2
    first, last = stage == 0, stage == pairs - 1
    modes, cells = blocks[0].shape[1:]
    terms = coeffs.shape[1]
    chunk = 16
    acc_shape = (modes, terms, 2 * modes)
    operands = [coeffs] + list(blocks)
    if stage >= pairs // 2:
        operands.append(halo)
    if not first:
        operands.append(before)
    scratch = [
        pltpu.VMEM((9, modes, cells), F32),
        pltpu.VMEM((9, terms, cells), F32),
        pltpu.VMEM((2 * modes, 4 * cells), BF16),
        pltpu.VMEM((2 * modes, 2 * cells), BF16),
    ]
    if last:
        part = jax.ShapeDtypeStruct(
            (n_space // 2, modes // n_space // 2, terms, 2 * modes), F32
        )
        out_shape = [part, part]
        scratch = [pltpu.VMEM(acc_shape, F32)] + scratch
    else:
        out_shape = jax.ShapeDtypeStruct(acc_shape, F32)
    whole = pl.BlockSpec(memory_space=pltpu.VMEM)
    return pl.pallas_call(
        functools.partial(stage_kernel, stage, first, last, n_term, n_space, chunk),
        out_shape=out_shape,
        in_specs=[whole] * len(operands),
        out_specs=[whole, whole] if last else whole,
        scratch_shapes=scratch,
        compiler_params=pltpu.CompilerParams(vmem_limit_bytes=40 << 20),
        cost_estimate=pl.CostEstimate(
            flops=2 * 2 * 2 * terms * modes * 2 * modes * cells,
            bytes_accessed=4 << 20,
            transcendentals=0,
        ),
    )(*operands)


def exchange(values, axis, apart):
    count = lax.axis_size(axis)
    return lax.ppermute(values, axis, [(i, i ^ apart) for i in range(count)])


def local(right_modes, adjoint_modes, conductivity_terms):
    n_term, n_space = lax.axis_size("term"), lax.axis_size("space")
    term_at, space_at = lax.axis_index("term"), lax.axis_index("space")
    pairs = n_term // 2
    z, y = term_at // 2, term_at % 2
    modes, cells = right_modes.shape[1:]
    terms = conductivity_terms.shape[1]

    own = jnp.concatenate([right_modes, adjoint_modes], 0)
    blocks = [own, exchange(own, "term", 1)]
    for stage in range(1, pairs):
        came = exchange(own, "term", 2 * stage)
        blocks += [came, exchange(came, "term", 1)]

    is_low = term_at < n_term // 2
    wanted = jnp.where(is_low, z, (pairs - 1) ^ z)
    takes_own = (y == 0) == is_low
    rim = blocks[0]
    for j in range(pairs // 2):
        block = jnp.where(takes_own, blocks[2 * j], blocks[2 * j + 1])
        rim = block if j == 0 else jnp.where(wanted == j, block, rim)
    rim_coeff = jnp.where(is_low, conductivity_terms[0], conductivity_terms[-1])
    rim = jnp.concatenate([rim.reshape(2 * modes, cells), rim_coeff], 0)
    route = []
    for s in range(n_space - 1):
        for t in range(n_term):
            low, high = s * n_term + t, (s + 1) * n_term + t
            route.append((high, low) if t < n_term // 2 else (low, high))
    halo = lax.ppermute(rim, ("space", "term"), route)

    value = None
    for stage in range(pairs):
        value = run_stage(
            stage, n_term, n_space, conductivity_terms, blocks[: 2 * stage + 2], halo, value
        )
    keep, send = value
    total = keep + exchange(send, "space", 1)
    apart = 2
    while apart < n_space:
        bit = space_at // apart % 2
        halves = total.reshape((total.shape[0] // 2, 2) + total.shape[1:])
        send = lax.dynamic_index_in_dim(halves, 1 - bit, 1, keepdims=False)
        keep = lax.dynamic_index_in_dim(halves, bit, 1, keepdims=False)
        total = keep + exchange(send, "space", apart)
        apart *= 2
    return jnp.transpose(total[0], (1, 0, 2)).reshape(terms, -1)


def solution(mesh):
    placed = (
        P(("space", "term"), None, None),
        P(("space", "term"), None, None),
        P("space", "term", None),
    )
    return jax.shard_map(
        local, mesh=mesh, in_specs=placed, out_specs=P("term", "space"), check_vma=False
    )
```

```python
import functools

import jax
import jax.numpy as jnp
from jax import lax
from jax.experimental import pallas as pl
from jax.experimental.pallas import tpu as pltpu
from jax.sharding import PartitionSpec as P

GY = 32
OFFSETS = (GY, -GY, 1, -1)
NT = (((1,), (1,)), ((), ()))
F32 = jnp.float32
BF16 = jnp.bfloat16


def shifted(values, offset):
    width = values.shape[-1]
    lane = lax.broadcasted_iota(jnp.int32, values.shape, values.ndim - 1)
    moved = pltpu.roll(values, (-offset) % width, values.ndim - 1)
    if offset == GY:
        keep = lane < width - GY
    elif offset == -GY:
        keep = lane >= GY
    elif offset == 1:
        keep = lane % GY != GY - 1
    else:
        keep = lane % GY != 0
    return jnp.where(keep, moved, 0.0)


def split(values):
    high = values.astype(BF16)
    return high, (values - high.astype(F32)).astype(BF16)


def stage_kernel(stage, first, last, n_term, n_space, *refs):
    k_ref = refs[0]
    blocks = refs[1 : 3 + 2 * stage]
    rest = list(refs[3 + 2 * stage :])
    pairs = n_term // 2
    far = stage >= pairs // 2
    halo_ref = rest.pop(0) if far else None
    before_ref = None if first else rest.pop(0)
    if last:
        keep_ref, send_ref, acc_ref = rest[:3]
        rest = rest[3:]
    else:
        acc_ref = rest.pop(0)
    da_ref, kb_ref, w_ref, dz_ref, kz_ref, wz_ref = rest
    modes = blocks[0].shape[1]
    terms = k_ref.shape[1]
    cells = k_ref.shape[2]
    group = 16
    term_at = lax.axis_index("term")
    space_at = lax.axis_index("space")
    z, y = term_at // 2, term_at % 2
    w = z ^ stage
    own_ref, other_ref = blocks[2 * stage], blocks[2 * stage + 1]

    coeffs = (k_ref[2 * w + y], k_ref[2 * w + 1 - y])
    fields = [ref[1] for ref in (own_ref, other_ref)]
    for m, ref in enumerate((own_ref, other_ref)):
        for d, offset in enumerate(OFFSETS):
            da_ref[4 * m + d] = fields[m] - shifted(fields[m], offset)
            kb_ref[4 * m + d] = 0.5 * (coeffs[m] + shifted(coeffs[m], offset))
        both = jnp.concatenate(split(ref[0]), 0)
        w_ref[:, 2 * m * cells : (2 * m + 1) * cells] = both
        w_ref[:, (2 * m + 1) * cells : (2 * m + 2) * cells] = both
    da_ref[8] = fields[0] - fields[1]
    kb_ref[8] = 0.5 * (coeffs[0] + coeffs[1])

    for r in range(0, modes, group):
        da = [da_ref[d, r : r + group, :] for d in range(9)]
        rows_a, rows_b = [], []
        for q in range(terms):
            part = [da[d] * kb_ref[d, q : q + 1, :] for d in range(9)]
            rows_a.append((part[0] + part[1]) + (part[2] + part[3]) + part[8])
            rows_b.append((part[4] + part[5]) + (part[6] + part[7]) - part[8])
        left = jnp.concatenate(
            split(jnp.concatenate(rows_a, 0)) + split(jnp.concatenate(rows_b, 0)), 1
        )
        out = lax.dot_general(left, w_ref[...], NT, preferred_element_type=F32)
        out = out.reshape(terms, group, 2 * modes)
        acc_ref[:, r : r + group] = out if first else before_ref[:, r : r + group] + out

    def edge(slot, here, there, coeff):
        dz_ref[slot] = here[1] - (0.0 if there is None else there[1])
        kz_ref[slot] = coeff
        both = jnp.concatenate(split(here[0] - (0.0 if there is None else there[0])), 0)
        wz_ref[slot, :, :cells] = both
        wz_ref[slot, :, cells:] = both

    count = 0
    for upward in (0, 1):
        near_w = w + 1 if upward else w - 1
        inside = (near_w >= 0) & (near_w < pairs)
        for j in range(stage):
            for parity in (0, 1):
                @pl.when(inside & (near_w ^ z == j) & (y == parity))
                def _(slot=count):
                    here = own_ref if parity == upward else other_ref
                    there = blocks[2 * j] if parity == 1 - upward else blocks[2 * j + 1]
                    plane = 2 * w + upward
                    edge(
                        slot,
                        here,
                        there,
                        0.5 * (k_ref[plane] + k_ref[plane + (1 if upward else -1)]),
                    )

        count = count + jnp.where(inside & (near_w ^ z < stage), 1, 0)

    is_low = term_at < n_term // 2
    for upward in (0, 1):
        at_rim = w == (pairs - 1 if upward else 0)
        plane = n_term - 1 if upward else 0
        near_side = jnp.logical_not(is_low) if upward else is_low
        if far:
            used = at_rim & jnp.logical_not(near_side)
        else:
            used = at_rim & near_side & (space_at == (n_space - 1 if upward else 0))
        for parity in (0, 1):
            @pl.when(used & (y == parity))
            def _(slot=count):
                here = own_ref if parity == upward else other_ref
                if far:
                    halo = halo_ref.at[: 2 * modes].reshape(2, modes, cells)
                    edge(slot, here, halo, 0.5 * (k_ref[plane] + halo_ref[2 * modes :]))
                else:
                    edge(slot, here, None, 0.5 * k_ref[plane])

        count = count + jnp.where(used, 1, 0)

    def layer(slot, carry):
        for r in range(0, modes, group):
            dz = dz_ref[slot, r : r + group, :]
            rows = [dz * kz_ref[slot, q : q + 1, :] for q in range(terms)]
            left = jnp.concatenate(split(jnp.concatenate(rows, 0)), 1)
            out = lax.dot_general(left, wz_ref[slot], NT, preferred_element_type=F32)
            acc_ref[:, r : r + group] += out.reshape(terms, group, 2 * modes)
        return carry

    lax.fori_loop(0, count, layer, 0)

    if last:
        core = space_at % 2
        lane = lax.broadcasted_iota(jnp.int32, (terms, 8, 2 * modes), 2)
        groups = []
        for r in range(0, modes, group):
            even = acc_ref[:, pl.ds(r, 8, stride=2), :]
            odd = acc_ref[:, pl.ds(r + 1, 8, stride=2), :]
            even = even + pltpu.roll(even, modes, 2)
            odd = odd + pltpu.roll(odd, modes, 2)
            groups.append(jnp.where(lane < modes, even, odd))
        packed = jnp.concatenate(groups, 1)
        width = packed.shape[1] // n_space
        for index in range(n_space // 2):
            low = packed[:, 2 * index * width : (2 * index + 1) * width]
            high = packed[:, (2 * index + 1) * width : (2 * index + 2) * width]
            keep_ref[index] = jnp.where(core == 0, low, high)
            send_ref[index] = jnp.where(core == 0, high, low)


def run_stage(stage, n_term, n_space, coeffs, blocks, halo, before):
    pairs = n_term // 2
    first, last = stage == 0, stage == pairs - 1
    modes, cells = blocks[0].shape[1:]
    terms = coeffs.shape[1]
    acc_shape = (terms, modes, 2 * modes)
    operands = [coeffs] + list(blocks)
    if stage >= pairs // 2:
        operands.append(halo)
    if not first:
        operands.append(before)
    scratch = [
        pltpu.VMEM((9, modes, cells), F32),
        pltpu.VMEM((9, terms, cells), F32),
        pltpu.VMEM((2 * modes, 4 * cells), BF16),
        pltpu.VMEM((3, modes, cells), F32),
        pltpu.VMEM((3, terms, cells), F32),
        pltpu.VMEM((3, 2 * modes, 2 * cells), BF16),
    ]
    if last:
        part = jax.ShapeDtypeStruct(
            (n_space // 2, terms, modes // n_space // 2, 2 * modes), F32
        )
        out_shape = [part, part]
        scratch = [pltpu.VMEM(acc_shape, F32)] + scratch
    else:
        out_shape = jax.ShapeDtypeStruct(acc_shape, F32)
    whole = pl.BlockSpec(memory_space=pltpu.VMEM)
    return pl.pallas_call(
        functools.partial(stage_kernel, stage, first, last, n_term, n_space),
        out_shape=out_shape,
        in_specs=[whole] * len(operands),
        out_specs=[whole, whole] if last else whole,
        scratch_shapes=scratch,
        compiler_params=pltpu.CompilerParams(vmem_limit_bytes=40 << 20),
        cost_estimate=pl.CostEstimate(
            flops=16 * 2 * 2 * 2 * terms * modes * 2 * modes * cells,
            bytes_accessed=4 << 20,
            transcendentals=0,
        ),
    )(*operands)


def exchange(values, axis, apart):
    count = lax.axis_size(axis)
    return lax.ppermute(values, axis, [(i, i ^ apart) for i in range(count)])


def local(right_modes, adjoint_modes, conductivity_terms):
    n_term, n_space = lax.axis_size("term"), lax.axis_size("space")
    term_at, space_at = lax.axis_index("term"), lax.axis_index("space")
    pairs = n_term // 2
    z, y = term_at // 2, term_at % 2
    modes, cells = right_modes.shape[1:]
    terms = conductivity_terms.shape[1]

    def after(x, *deps):
        return lax.optimization_barrier((x,) + deps)[0]

    def go(stage, before, halo=None):
        return run_stage(stage, n_term, n_space, conductivity_terms, blocks[: 2 * stage + 2], halo, before)

    which = lax.broadcasted_iota(jnp.int32, (2, 1, 1), 0)
    own = jnp.where(which == 0, right_modes, adjoint_modes)
    half = pairs // 2
    column = {half: exchange(own, "term", 2 * half)}
    blocks = [own, exchange(own, "term", 1)]
    for stage in range(1, half):
        column[stage] = exchange(own, "term", 2 * stage)
    for stage in range(half + 1, pairs):
        column[stage] = exchange(after(own, blocks[1]), "term", 2 * stage)
    value = go(0, None)
    for stage in range(1, half):
        came = after(column[stage], value)
        blocks += [came, exchange(came, "term", 1)]
    came = after(column[half], blocks[2 * half - 1])
    ahead = [came, exchange(came, "term", 1)]
    for stage in range(1, half):
        value = go(stage, value)
    for stage in range(half + 1, pairs):
        came = after(column[stage], value)
        ahead += [came, exchange(came, "term", 1)]
    blocks += ahead

    is_low = term_at < n_term // 2
    wanted = jnp.where(is_low, z, (pairs - 1) ^ z)
    takes_own = (y == 0) == is_low
    rim = blocks[0]
    for j in range(pairs // 2):
        block = jnp.where(takes_own, blocks[2 * j], blocks[2 * j + 1])
        rim = block if j == 0 else jnp.where(wanted == j, block, rim)
    rim_coeff = jnp.where(is_low, conductivity_terms[0], conductivity_terms[-1])
    rim = jnp.concatenate([rim.reshape(2 * modes, cells), rim_coeff], 0)
    route = []
    for s in range(n_space - 1):
        for t in range(n_term):
            low, high = s * n_term + t, (s + 1) * n_term + t
            route.append((high, low) if t < n_term // 2 else (low, high))
    halo = lax.ppermute(rim, ("space", "term"), route)

    for stage in range(half, pairs):
        value = go(stage, value, halo)
    keep, send = value
    total = keep + exchange(send, "space", 1)
    apart = 2
    while apart < n_space:
        bit = space_at // apart % 2
        halves = total.reshape((total.shape[0] // 2, 2) + total.shape[1:])
        send = lax.dynamic_index_in_dim(halves, 1 - bit, 1, keepdims=False)
        keep = lax.dynamic_index_in_dim(halves, bit, 1, keepdims=False)
        total = keep + exchange(send, "space", apart)
        apart *= 2
    return total[0].reshape(terms, -1)


def solution(mesh):
    placed = (
        P(("space", "term"), None, None),
        P(("space", "term"), None, None),
        P("space", "term", None),
    )
    return jax.shard_map(
        local, mesh=mesh, in_specs=placed, out_specs=P("term", "space"), check_vma=False
    )
```

```python
import functools

import jax
import jax.numpy as jnp
from jax import lax
from jax.experimental import pallas as pl
from jax.experimental.pallas import tpu as pltpu
from jax.sharding import PartitionSpec as P

GY = 32
OFFSETS = (GY, -GY, 1, -1)
NT = (((1,), (1,)), ((), ()))
F32 = jnp.float32
BF16 = jnp.bfloat16


def shifted(values, offset):
    width = values.shape[-1]
    lane = lax.broadcasted_iota(jnp.int32, values.shape, values.ndim - 1)
    moved = pltpu.roll(values, (-offset) % width, values.ndim - 1)
    if offset == GY:
        keep = lane < width - GY
    elif offset == -GY:
        keep = lane >= GY
    elif offset == 1:
        keep = lane % GY != GY - 1
    else:
        keep = lane % GY != 0
    return jnp.where(keep, moved, 0.0)


def split(values):
    high = values.astype(BF16)
    return high, (values - high.astype(F32)).astype(BF16)


def stage_kernel(stage, first, last, n_term, n_space, *refs):
    k_ref = refs[0]
    blocks = refs[1 : 3 + 2 * stage]
    rest = list(refs[3 + 2 * stage :])
    pairs = n_term // 2
    far = stage >= pairs // 2
    halo_ref = rest.pop(0) if far else None
    before_ref = None if first else rest.pop(0)
    if last:
        keep_ref, send_ref, acc_ref = rest[:3]
        rest = rest[3:]
    else:
        acc_ref = rest.pop(0)
    da_ref, kb_ref, w_ref, dz_ref, kz_ref, wz_ref = rest
    modes = blocks[0].shape[1]
    terms = k_ref.shape[1]
    cells = k_ref.shape[2]
    group = 16
    term_at = lax.axis_index("term")
    space_at = lax.axis_index("space")
    z, y = term_at // 2, term_at % 2
    w = z ^ stage
    own_ref, other_ref = blocks[2 * stage], blocks[2 * stage + 1]

    coeffs = (k_ref[2 * w + y], k_ref[2 * w + 1 - y])
    fields = [ref[1] for ref in (own_ref, other_ref)]
    for m, ref in enumerate((own_ref, other_ref)):
        for d, offset in enumerate(OFFSETS):
            da_ref[4 * m + d] = fields[m] - shifted(fields[m], offset)
            kb_ref[4 * m + d] = 0.5 * (coeffs[m] + shifted(coeffs[m], offset))
        both = jnp.concatenate(split(ref[0]), 0)
        w_ref[:, 2 * m * cells : (2 * m + 1) * cells] = both
        w_ref[:, (2 * m + 1) * cells : (2 * m + 2) * cells] = both
    da_ref[8] = fields[0] - fields[1]
    kb_ref[8] = 0.5 * (coeffs[0] + coeffs[1])

    for r in range(0, modes, group):
        da = [da_ref[d, r : r + group, :] for d in range(9)]
        rows_a, rows_b = [], []
        for q in range(terms):
            part = [da[d] * kb_ref[d, q : q + 1, :] for d in range(9)]
            rows_a.append((part[0] + part[1]) + (part[2] + part[3]) + part[8])
            rows_b.append((part[4] + part[5]) + (part[6] + part[7]) - part[8])
        left = jnp.concatenate(
            split(jnp.concatenate(rows_a, 0)) + split(jnp.concatenate(rows_b, 0)), 1
        )
        out = lax.dot_general(left, w_ref[...], NT, preferred_element_type=F32)
        out = out.reshape(terms, group, 2 * modes)
        acc_ref[:, r : r + group] = out if first else before_ref[:, r : r + group] + out

    def edge(slot, here, there, coeff):
        dz_ref[slot] = here[1] - (0.0 if there is None else there[1])
        kz_ref[slot] = coeff
        both = jnp.concatenate(split(here[0] - (0.0 if there is None else there[0])), 0)
        wz_ref[slot, :, :cells] = both
        wz_ref[slot, :, cells:] = both

    count = 0
    for upward in (0, 1):
        near_w = w + 1 if upward else w - 1
        inside = (near_w >= 0) & (near_w < pairs)
        for j in range(stage):
            for parity in (0, 1):
                @pl.when(inside & (near_w ^ z == j) & (y == parity))
                def _(slot=count):
                    here = own_ref if parity == upward else other_ref
                    there = blocks[2 * j] if parity == 1 - upward else blocks[2 * j + 1]
                    plane = 2 * w + upward
                    edge(
                        slot,
                        here,
                        there,
                        0.5 * (k_ref[plane] + k_ref[plane + (1 if upward else -1)]),
                    )

        count = count + jnp.where(inside & (near_w ^ z < stage), 1, 0)

    is_low = term_at < n_term // 2
    for upward in (0, 1):
        at_rim = w == (pairs - 1 if upward else 0)
        plane = n_term - 1 if upward else 0
        near_side = jnp.logical_not(is_low) if upward else is_low
        if far:
            used = at_rim & jnp.logical_not(near_side)
        else:
            used = at_rim & near_side & (space_at == (n_space - 1 if upward else 0))
        for parity in (0, 1):
            @pl.when(used & (y == parity))
            def _(slot=count):
                here = own_ref if parity == upward else other_ref
                if far:
                    inner = space_at != (n_space - 1 if upward else 0)
                    came = jnp.where(inner, halo_ref[...], 0.0)
                    halo = (came[:modes], came[modes : 2 * modes])
                    edge(slot, here, halo, 0.5 * (k_ref[plane] + came[2 * modes :]))
                else:
                    edge(slot, here, None, 0.5 * k_ref[plane])

        count = count + jnp.where(used, 1, 0)

    def layer(slot, carry):
        for r in range(0, modes, group):
            dz = dz_ref[slot, r : r + group, :]
            rows = [dz * kz_ref[slot, q : q + 1, :] for q in range(terms)]
            left = jnp.concatenate(split(jnp.concatenate(rows, 0)), 1)
            out = lax.dot_general(left, wz_ref[slot], NT, preferred_element_type=F32)
            acc_ref[:, r : r + group] += out.reshape(terms, group, 2 * modes)
        return carry

    lax.fori_loop(0, count, layer, 0)

    if last:
        core = space_at % 2
        lane = lax.broadcasted_iota(jnp.int32, (terms, 8, 2 * modes), 2)
        groups = []
        for r in range(0, modes, group):
            even = acc_ref[:, pl.ds(r, 8, stride=2), :]
            odd = acc_ref[:, pl.ds(r + 1, 8, stride=2), :]
            even = even + pltpu.roll(even, modes, 2)
            odd = odd + pltpu.roll(odd, modes, 2)
            groups.append(jnp.where(lane < modes, even, odd))
        packed = jnp.concatenate(groups, 1)
        width = packed.shape[1] // n_space
        for index in range(n_space // 2):
            low = packed[:, 2 * index * width : (2 * index + 1) * width]
            high = packed[:, (2 * index + 1) * width : (2 * index + 2) * width]
            keep_ref[index] = jnp.where(core == 0, low, high)
            send_ref[index] = jnp.where(core == 0, high, low)


def run_stage(stage, n_term, n_space, coeffs, blocks, halo, before):
    pairs = n_term // 2
    first, last = stage == 0, stage == pairs - 1
    modes, cells = blocks[0].shape[1:]
    terms = coeffs.shape[1]
    acc_shape = (terms, modes, 2 * modes)
    operands = [coeffs] + list(blocks)
    if stage >= pairs // 2:
        operands.append(halo)
    if not first:
        operands.append(before)
    scratch = [
        pltpu.VMEM((9, modes, cells), F32),
        pltpu.VMEM((9, terms, cells), F32),
        pltpu.VMEM((2 * modes, 4 * cells), BF16),
        pltpu.VMEM((3, modes, cells), F32),
        pltpu.VMEM((3, terms, cells), F32),
        pltpu.VMEM((3, 2 * modes, 2 * cells), BF16),
    ]
    if last:
        part = jax.ShapeDtypeStruct(
            (n_space // 2, terms, modes // n_space // 2, 2 * modes), F32
        )
        out_shape = [part, part]
        scratch = [pltpu.VMEM(acc_shape, F32)] + scratch
    else:
        out_shape = jax.ShapeDtypeStruct(acc_shape, F32)
    whole = pl.BlockSpec(memory_space=pltpu.VMEM)
    return pl.pallas_call(
        functools.partial(stage_kernel, stage, first, last, n_term, n_space),
        out_shape=out_shape,
        in_specs=[whole] * len(operands),
        out_specs=[whole, whole] if last else whole,
        scratch_shapes=scratch,
        compiler_params=pltpu.CompilerParams(vmem_limit_bytes=40 << 20),
        cost_estimate=pl.CostEstimate(
            flops=1 * 2 * 2 * 2 * terms * modes * 2 * modes * cells,
            bytes_accessed=4 << 20,
            transcendentals=0,
        ),
    )(*operands)


def exchange(values, axis, apart):
    count = lax.axis_size(axis)
    return lax.ppermute(values, axis, [(i, i ^ apart) for i in range(count)])


def local(right_modes, adjoint_modes, conductivity_terms):
    n_term, n_space = lax.axis_size("term"), lax.axis_size("space")
    term_at, space_at = lax.axis_index("term"), lax.axis_index("space")
    pairs = n_term // 2
    z, y = term_at // 2, term_at % 2
    modes, cells = right_modes.shape[1:]
    terms = conductivity_terms.shape[1]

    def after(x, *deps):
        return lax.optimization_barrier((x,) + deps)[0]

    def go(stage, before, halo=None):
        return run_stage(stage, n_term, n_space, conductivity_terms, blocks[: 2 * stage + 2], halo, before)

    which = lax.broadcasted_iota(jnp.int32, (2, 1, 1), 0)
    own = jnp.where(which == 0, right_modes, adjoint_modes)
    half = pairs // 2
    column = {}
    column[half] = exchange(own, "term", 2 * half)
    for stage in range(1, half):
        column[stage] = exchange(own, "term", 2 * stage)
        column[half + stage] = exchange(column[half], "term", 2 * stage)
    blocks = [own, exchange(own, "term", 1)]
    for stage in range(1, half):
        blocks += [column[stage], exchange(column[stage], "term", 1)]
    ahead = [column[half], exchange(column[half], "term", 1)]
    value = go(0, None)
    first_value = value
    blocks = blocks[:2] + [after(x, value) for x in blocks[2:]]
    for stage in range(1, half):
        value = go(stage, value)
    for stage in range(half + 1, pairs):
        came = after(column[stage], value)
        ahead += [came, exchange(came, "term", 1)]
    blocks += ahead

    is_low = term_at < n_term // 2
    wanted = jnp.where(is_low, z, (pairs - 1) ^ z)
    takes_own = (y == 0) == is_low
    rim = after(blocks[0], first_value)
    for j in range(pairs // 2):
        block = jnp.where(takes_own, blocks[2 * j], blocks[2 * j + 1])
        rim = block if j == 0 else jnp.where(wanted == j, block, rim)
    rim_coeff = jnp.where(is_low, conductivity_terms[0], conductivity_terms[-1])
    rim = jnp.concatenate([rim.reshape(2 * modes, cells), rim_coeff], 0)
    route = []
    for s in range(n_space):
        for t in range(n_term):
            low, high = s * n_term + t, (s + 1) % n_space * n_term + t
            route.append((high, low) if t < n_term // 2 else (low, high))
    halo = lax.ppermute(rim, ("space", "term"), route)

    for stage in range(half, pairs):
        value = go(stage, value, halo)
    keep, send = value
    total = keep + exchange(send, "space", 1)
    apart = 2
    while apart < n_space:
        bit = space_at // apart % 2
        halves = total.reshape((total.shape[0] // 2, 2) + total.shape[1:])
        send = lax.dynamic_index_in_dim(halves, 1 - bit, 1, keepdims=False)
        keep = lax.dynamic_index_in_dim(halves, bit, 1, keepdims=False)
        total = keep + exchange(send, "space", apart)
        apart *= 2
    return total[0].reshape(terms, -1)


def solution(mesh):
    placed = (
        P(("space", "term"), None, None),
        P(("space", "term"), None, None),
        P("space", "term", None),
    )
    return jax.shard_map(
        local, mesh=mesh, in_specs=placed, out_specs=P("term", "space"), check_vma=False
    )
```

```python
import functools

import jax
import jax.numpy as jnp
from jax import lax
from jax.experimental import pallas as pl
from jax.experimental.pallas import tpu as pltpu
from jax.sharding import PartitionSpec as P

GY = 32
GROUP = 16
OFFSETS = (GY, -GY, 1, -1)
NT = (((1,), (1,)), ((), ()))
F32 = jnp.float32
BF16 = jnp.bfloat16


def shifted(values, offset):
    width = values.shape[-1]
    lane = lax.broadcasted_iota(jnp.int32, values.shape, values.ndim - 1)
    moved = pltpu.roll(values, (-offset) % width, values.ndim - 1)
    if offset == GY:
        keep = lane < width - GY
    elif offset == -GY:
        keep = lane >= GY
    elif offset == 1:
        keep = lane % GY != GY - 1
    else:
        keep = lane % GY != 0
    return jnp.where(keep, moved, 0.0)


def split(values):
    high = values.astype(BF16)
    return high, (values - high.astype(F32)).astype(BF16)


def pair_kernel(stage, n_term, n_space, first, extra, *refs):
    pairs = n_term // 2
    far = stage >= pairs // 2
    k_ref = refs[0]
    count = 2 * stage + 2 + extra
    blocks = refs[1 : 1 + count]
    rest = list(refs[1 + count :])
    halo_ref = rest.pop(0) if far else None
    before_ref = None if first else rest.pop(0)
    acc_ref, da_ref, kb_ref, w_ref, dz_ref, kz_ref, wz_ref = rest
    modes, cells = blocks[0].shape[1:]
    terms = k_ref.shape[1]
    term_at = lax.axis_index("term")
    z, y = term_at // 2, term_at % 2
    w = z ^ stage
    own_ref, other_ref = blocks[2 * stage], blocks[2 * stage + 1]
    linked = 1 if stage == 1 else 0 if stage == 0 else 1 + extra if pairs == 4 else 2 + extra

    def weights(slot, values):
        both = jnp.concatenate(split(values), 0)
        w_ref[slot] = jnp.concatenate([both, both], 1)

    in_plane = [(own_ref, 2 * w + y), (other_ref, 2 * w + 1 - y)]
    if extra:
        in_plane.append((blocks[-1], 2 * (z ^ (pairs - 1)) + y))
    for m, (ref, plane) in enumerate(in_plane):
        a, k = ref[1], k_ref[plane]
        for d, offset in enumerate(OFFSETS):
            da_ref[4 * m + d] = a - shifted(a, offset)
            kb_ref[4 * m + d] = 0.5 * (k + shifted(k, offset))
        weights(m, ref[0])
    across = 4 * len(in_plane)
    da_ref[across] = own_ref[1] - other_ref[1]
    kb_ref[across] = 0.5 * (k_ref[2 * w + y] + k_ref[2 * w + 1 - y])
    link = across + 1
    if stage > 1:
        def edge(slot, here, there, coeff):
            da_ref[link + slot] = here[1] - there[1]
            kb_ref[link + slot] = coeff
            both = jnp.concatenate(split(here[0] - there[0]), 0)
            w_ref[len(in_plane) + slot] = jnp.concatenate([both, both], 1)

        slot = 0
        visits = [(stage, (0, 1))] + [(pairs - 1, (0,))] * extra
        for at, sides in visits:
            slot = edges(at, sides, slot, n_term, n_space, k_ref, blocks, halo_ref, edge)
        for index in range(linked):
            @pl.when(slot <= index)
            def _():
                da_ref[link + index] = jnp.zeros((modes, cells), F32)
                kb_ref[link + index] = jnp.zeros((terms, cells), F32)
                w_ref[len(in_plane) + index] = jnp.zeros((2 * modes, 2 * cells), BF16)

    if stage == 1:
        upward = jnp.where(w % 2 == 0, 1, 0)
        for direction in (0, 1):
            for parity in (0, 1):
                @pl.when((upward == direction) & (y == parity))
                def _():
                    here = own_ref if parity == direction else other_ref
                    there = blocks[0] if parity == 1 - direction else blocks[1]
                    da_ref[link] = here[1] - there[1]
                    weights(len(in_plane), here[0] - there[0])

        kb_ref[link] = 0.5 * (k_ref[2 * w + upward] + k_ref[2 * w + 3 * upward - 1])

    for r in range(0, modes, GROUP):
        rows = [[] for _ in range(len(in_plane) + linked)]
        da = [da_ref[d, r : r + GROUP, :] for d in range(across + 1 + linked)]
        for q in range(terms):
            part = [da[d] * kb_ref[d, q : q + 1, :] for d in range(across + 1 + linked)]
            for m in range(len(in_plane)):
                total = (part[4 * m] + part[4 * m + 1]) + (part[4 * m + 2] + part[4 * m + 3])
                if m == 0:
                    total = total + part[across]
                elif m == 1:
                    total = total - part[across]
                rows[m].append(total)
            for index in range(linked):
                rows[len(in_plane) + index].append(part[link + index])
        out = product(rows, jnp.concatenate([w_ref[m] for m in range(len(rows))], 1))
        out = out.reshape(terms, GROUP, 2 * modes)
        acc_ref[:, r : r + GROUP] = out if first else before_ref[:, r : r + GROUP] + out

    if stage > 1:
        return

    def edge(slot, here, there, coeff):
        dz_ref[...] = here[1] - there[1]
        kz_ref[...] = coeff
        both = jnp.concatenate(split(here[0] - there[0]), 0)
        wz_ref[...] = jnp.concatenate([both, both], 1)

    slot = edges(stage, (0, 1), 0, n_term, n_space, k_ref, blocks, halo_ref, edge, skip=True)

    @pl.when(slot > 0)
    def _():
        for r in range(0, modes, GROUP):
            dz = dz_ref[r : r + GROUP, :]
            rows = [[dz * kz_ref[q : q + 1, :] for q in range(terms)]]
            out = product(rows, wz_ref[...])
            acc_ref[:, r : r + GROUP] += out.reshape(terms, GROUP, 2 * modes)


def product(rows, weights):
    left = []
    for part in rows:
        left += split(jnp.concatenate(part, 0))
    return lax.dot_general(jnp.concatenate(left, 1), weights, NT, preferred_element_type=F32)


def edges(stage, sides, slot, n_term, n_space, k_ref, blocks, halo_ref, edge, skip=False):
    pairs = n_term // 2
    modes = blocks[0].shape[1]
    term_at, space_at = lax.axis_index("term"), lax.axis_index("space")
    z, y = term_at // 2, term_at % 2
    w = z ^ stage
    far = stage >= pairs // 2
    is_low = term_at < n_term // 2
    for upward in (0, 1):
        near_w = w + 1 if upward else w - 1
        inside = (near_w >= 0) & (near_w < pairs) & (near_w ^ z < stage)
        for parity in (0, 1):
            side = 0 if parity == upward else 1
            if side not in sides:
                continue
            here = blocks[2 * stage + side]
            mine = y == parity
            if not skip:
                for j in range(stage):
                    @pl.when(inside & mine & (near_w ^ z == j))
                    def _(slot=slot):
                        plane = 2 * w + upward
                        beyond = plane + (1 if upward else -1)
                        edge(slot, here, blocks[2 * j + 1 - side], 0.5 * (k_ref[plane] + k_ref[beyond]))

                slot = slot + jnp.where(inside & mine, 1, 0)
            used = mine & (w == (pairs - 1 if upward else 0))
            plane = n_term - 1 if upward else 0
            edge_space = space_at == (n_space - 1 if upward else 0)
            if far:
                used = used & (is_low if upward else jnp.logical_not(is_low))
            else:
                used = used & (jnp.logical_not(is_low) if upward else is_low) & edge_space

            @pl.when(used)
            def _(slot=slot):
                if far:
                    came = jnp.where(edge_space, 0.0, halo_ref[...])
                    halo = (came[:modes], came[modes : 2 * modes])
                    edge(slot, here, halo, 0.5 * (k_ref[plane] + came[2 * modes :]))
                else:
                    edge(slot, here, (0.0, 0.0), 0.5 * k_ref[plane])

            slot = slot + jnp.where(used, 1, 0)
    return slot


def last_kernel(n_term, n_space, mine, *refs):
    pairs = n_term // 2
    k_ref, blocks, rest = refs[0], refs[1 : 1 + n_term], refs[1 + n_term :]
    halo_ref, before_ref, keep_ref, send_ref, acc_ref, da_ref, kb_ref, w_ref = rest
    modes, cells = blocks[0].shape[1:]
    terms = k_ref.shape[1]
    term_at, space_at = lax.axis_index("term"), lax.axis_index("space")
    z, y = term_at // 2, term_at % 2
    w = z ^ (pairs - 1)
    column_ref, other_ref = blocks[-2], blocks[-1]
    a, k = other_ref[1], k_ref[2 * w + 1 - y]
    for d, offset in enumerate(OFFSETS):
        da_ref[d] = a - shifted(a, offset)
        kb_ref[d] = 0.5 * (k + shifted(k, offset))

    def weights(slot, values):
        both = jnp.concatenate(split(values), 0)
        at = 2 * slot * cells
        w_ref[:, at : at + cells] = both
        w_ref[:, at + cells : at + 2 * cells] = both

    weights(0, other_ref[0])
    da_ref[4] = a - column_ref[1]
    kb_ref[4] = 0.5 * (k + k_ref[2 * w + y])
    weights(1, other_ref[0] - column_ref[0])

    def edge(slot, here, there, coeff):
        da_ref[5] = here[1] - there[1]
        kb_ref[5] = coeff
        weights(2, here[0] - there[0])

    edges(pairs - 1, (1,), 0, n_term, n_space, k_ref, blocks, halo_ref, edge)

    side = space_at // 2 % 2
    side = side if mine else 1 - side
    width = modes // n_space
    size = 2 * width
    step = min(GROUP, size)
    for index in range(n_space // 4):
        for r in range(0, size, step):
            start = pl.multiple_of((2 * index + side) * size + r, step)
            da = [da_ref[d, pl.ds(start, step), :] for d in range(6)]
            rows = [[], [], []]
            for q in range(terms):
                part = [da[d] * kb_ref[d, q : q + 1, :] for d in range(6)]
                rows[0].append((part[0] + part[1]) + (part[2] + part[3]))
                rows[1].append(part[4])
                rows[2].append(part[5])
            out = product(rows, w_ref[...]).reshape(terms, step, 2 * modes)
            at = index * size + r
            acc_ref[:, at : at + step] = before_ref[:, pl.ds(start, step)] + out

    core = space_at % 2
    flat_ref = acc_ref.reshape(terms * (modes // 2), 2 * modes)
    lane = lax.broadcasted_iota(jnp.int32, (terms, 2 * modes), 1)
    for index in range(n_space // 4):
        for j in range(width // 2):
            packed = []
            for at in (index * size + 2 * j, index * size + width + 2 * j):
                even = flat_ref[pl.ds(at, terms, stride=modes // 2), :]
                odd = flat_ref[pl.ds(at + 1, terms, stride=modes // 2), :]
                even = even + pltpu.roll(even, modes, 1)
                odd = odd + pltpu.roll(odd, modes, 1)
                packed.append(jnp.where(lane < modes, even, odd))
            to = slice(2 * modes * j, 2 * modes * (j + 1))
            keep_ref[index, :, to] = jnp.where(core == 0, packed[0], packed[1])
            send_ref[index, :, to] = jnp.where(core == 0, packed[1], packed[0])


def call(kernel, operands, out_shape, scratch, flops=1 << 29):
    whole = pl.BlockSpec(memory_space=pltpu.VMEM)
    return pl.pallas_call(
        kernel,
        out_shape=out_shape,
        in_specs=[whole] * len(operands),
        out_specs=jax.tree.map(lambda _: whole, out_shape),
        scratch_shapes=scratch,
        compiler_params=pltpu.CompilerParams(vmem_limit_bytes=40 << 20),
        cost_estimate=pl.CostEstimate(flops=flops, bytes_accessed=flops >> 7, transcendentals=0),
    )(*operands)


def run_pair(stage, n_term, n_space, coeffs, blocks, halo, before):
    modes, cells = blocks[0].shape[1:]
    terms = coeffs.shape[1]
    extra = len(blocks) - 2 * stage - 2
    operands = [coeffs] + list(blocks)
    if halo is not None:
        operands.append(halo)
    if before is not None:
        operands.append(before)
    kernel = functools.partial(pair_kernel, stage, n_term, n_space, before is None, extra)
    scratch = [
        pltpu.VMEM((16, modes, cells), F32),
        pltpu.VMEM((16, terms, cells), F32),
        pltpu.VMEM((6, 2 * modes, 2 * cells), BF16),
        pltpu.VMEM((modes, cells), F32),
        pltpu.VMEM((terms, cells), F32),
        pltpu.VMEM((2 * modes, 2 * cells), BF16),
    ]
    shape = jax.ShapeDtypeStruct((terms, modes, 2 * modes), F32)
    return call(kernel, operands, shape, scratch)


def run_last(mine, n_term, n_space, coeffs, blocks, halo, before):
    modes, cells = blocks[0].shape[1:]
    terms = coeffs.shape[1]
    scratch = [
        pltpu.VMEM((terms, modes // 2, 2 * modes), F32),
        pltpu.VMEM((6, modes, cells), F32),
        pltpu.VMEM((6, terms, cells), F32),
        pltpu.VMEM((2 * modes, 6 * cells), BF16),
    ]
    shape = jax.ShapeDtypeStruct((n_space // 4, terms, modes * modes // n_space), F32)
    kernel = functools.partial(last_kernel, n_term, n_space, mine)
    return call(kernel, [coeffs] + list(blocks) + [halo, before], [shape, shape], scratch, 0 if mine else 1 << 29)


def exchange(values, axis, apart):
    count = lax.axis_size(axis)
    return lax.ppermute(values, axis, [(i, i ^ apart) for i in range(count)])


def local(right_modes, adjoint_modes, conductivity_terms):
    n_term, n_space = lax.axis_size("term"), lax.axis_size("space")
    term_at, space_at = lax.axis_index("term"), lax.axis_index("space")
    pairs = n_term // 2
    z, y = term_at // 2, term_at % 2
    modes, cells = right_modes.shape[1:]
    terms = conductivity_terms.shape[1]

    def after(x, *deps):
        return lax.optimization_barrier((x,) + deps)[0]

    def go(stage, before, halo=None):
        seen = blocks[: 2 * stage + 2]
        if stage == pairs - 2:
            seen = seen + [blocks[-2]]
        return run_pair(stage, n_term, n_space, conductivity_terms, seen, halo, before)

    which = lax.broadcasted_iota(jnp.int32, (2, 1, 1), 0)
    own = jnp.where(which == 0, right_modes, adjoint_modes)
    half = pairs // 2
    column = {}
    column[half] = exchange(own, "term", 2 * half)
    for stage in range(1, half):
        column[stage] = exchange(own, "term", 2 * stage)
        column[half + stage] = exchange(column[half], "term", 2 * stage)
    blocks = [own, exchange(own, "term", 1)]
    for stage in range(1, half):
        blocks += [column[stage], exchange(column[stage], "term", 1)]
    ahead = [column[half], exchange(column[half], "term", 1)]
    value = go(0, None)
    first_value = value
    blocks = blocks[:2] + [after(x, value) for x in blocks[2:]]
    for stage in range(1, half):
        value = go(stage, value)
    for stage in range(half + 1, pairs):
        came = after(column[stage], value)
        ahead += [came, exchange(came, "term", 1)]
    blocks += ahead

    is_low = term_at < n_term // 2
    wanted = jnp.where(is_low, z, (pairs - 1) ^ z)
    takes_own = (y == 0) == is_low
    rim = after(blocks[0], first_value)
    for j in range(pairs // 2):
        block = jnp.where(takes_own, blocks[2 * j], blocks[2 * j + 1])
        rim = block if j == 0 else jnp.where(wanted == j, block, rim)
    rim_coeff = jnp.where(is_low, conductivity_terms[0], conductivity_terms[-1])
    rim = jnp.concatenate([rim.reshape(2 * modes, cells), rim_coeff], 0)
    route = []
    for s in range(n_space):
        for t in range(n_term):
            low, high = s * n_term + t, (s + 1) % n_space * n_term + t
            route.append((high, low) if t < n_term // 2 else (low, high))
    halo = lax.ppermute(rim, ("space", "term"), route)

    for stage in range(half, pairs - 1):
        value = go(stage, value, halo)
    arguments = (n_term, n_space, conductivity_terms, blocks, halo, value)
    keep, send = run_last(False, *arguments)
    leaving = keep + exchange(send, "space", 1)
    away = exchange(leaving, "space", 2)
    value = after(value, leaving)
    keep, send = run_last(True, n_term, n_space, conductivity_terms, blocks, halo, value)
    middle = terms // 2
    came = [exchange(send[:, :middle], "space", 1), exchange(send[:, middle:], "space", 1)]
    total = keep + jnp.concatenate(came, 1) + away
    apart = 4
    while apart < n_space:
        bit = space_at // apart % 2
        halves = total.reshape((total.shape[0] // 2, 2) + total.shape[1:])
        send = lax.dynamic_index_in_dim(halves, 1 - bit, 1, keepdims=False)
        keep = lax.dynamic_index_in_dim(halves, bit, 1, keepdims=False)
        total = keep + exchange(send, "space", apart)
        apart *= 2
    return total[0]


def solution(mesh):
    placed = (
        P(("space", "term"), None, None),
        P(("space", "term"), None, None),
        P("space", "term", None),
    )
    return jax.shard_map(
        local, mesh=mesh, in_specs=placed, out_specs=P("term", "space"), check_vma=False
    )
```

```python
import functools

import jax
import jax.numpy as jnp
from jax import lax
from jax.experimental import pallas as pl
from jax.experimental.pallas import tpu as pltpu
from jax.sharding import PartitionSpec as P

GY = 32
GROUP = 16
OFFSETS = (GY, -GY, 1, -1)
NT = (((1,), (1,)), ((), ()))
F32 = jnp.float32
BF16 = jnp.bfloat16


def shifted(values, offset):
    width = values.shape[-1]
    lane = lax.broadcasted_iota(jnp.int32, values.shape, values.ndim - 1)
    moved = pltpu.roll(values, (-offset) % width, values.ndim - 1)
    if offset == GY:
        keep = lane < width - GY
    elif offset == -GY:
        keep = lane >= GY
    elif offset == 1:
        keep = lane % GY != GY - 1
    else:
        keep = lane % GY != 0
    return jnp.where(keep, moved, 0.0)


def split(values):
    high = values.astype(BF16)
    return high, (values - high.astype(F32)).astype(BF16)


def pair_kernel(stage, n_term, n_space, first, extra, *refs):
    pairs = n_term // 2
    far = stage >= pairs // 2
    k_ref = refs[0]
    count = 2 * stage + 2 + extra
    blocks = refs[1 : 1 + count]
    rest = list(refs[1 + count :])
    halo_ref = rest.pop(0) if far else None
    before_ref = None if first else rest.pop(0)
    acc_ref, da_ref, kb_ref, w_ref, dz_ref, kz_ref, wz_ref = rest
    modes, cells = blocks[0].shape[1:]
    terms = k_ref.shape[1]
    term_at = lax.axis_index("term")
    z, y = term_at // 2, term_at % 2
    w = z ^ stage
    own_ref, other_ref = blocks[2 * stage], blocks[2 * stage + 1]
    linked = 1 if stage == 1 else 0 if stage == 0 else 1 + extra if pairs == 4 else 2 + extra

    def weights(slot, values):
        both = jnp.concatenate(split(values), 0)
        w_ref[slot] = jnp.concatenate([both, both], 1)

    in_plane = [(own_ref, 2 * w + y), (other_ref, 2 * w + 1 - y)]
    if extra:
        in_plane.append((blocks[-1], 2 * (z ^ (pairs - 1)) + y))
    for m, (ref, plane) in enumerate(in_plane):
        a, k = ref[1], k_ref[plane]
        for d, offset in enumerate(OFFSETS):
            da_ref[4 * m + d] = a - shifted(a, offset)
            kb_ref[4 * m + d] = 0.5 * (k + shifted(k, offset))
        weights(m, ref[0])
    across = 4 * len(in_plane)
    da_ref[across] = own_ref[1] - other_ref[1]
    kb_ref[across] = 0.5 * (k_ref[2 * w + y] + k_ref[2 * w + 1 - y])
    link = across + 1
    if stage > 1:
        def edge(slot, here, there, coeff):
            da_ref[link + slot] = here[1] - there[1]
            kb_ref[link + slot] = coeff
            both = jnp.concatenate(split(here[0] - there[0]), 0)
            w_ref[len(in_plane) + slot] = jnp.concatenate([both, both], 1)

        slot = edges(stage, (0, 1), 0, n_term, n_space, k_ref, blocks, halo_ref, edge)
        if extra:
            edges(pairs - 1, (0,), linked - 1, n_term, n_space, k_ref, blocks, halo_ref, edge, fixed=True)
        for index in range(linked - extra):
            @pl.when(slot <= index)
            def _():
                da_ref[link + index] = jnp.zeros((modes, cells), F32)
                kb_ref[link + index] = jnp.zeros((terms, cells), F32)
                w_ref[len(in_plane) + index] = jnp.zeros((2 * modes, 2 * cells), BF16)

    if stage == 1:
        upward = jnp.where(w % 2 == 0, 1, 0)
        for direction in (0, 1):
            for parity in (0, 1):
                @pl.when((upward == direction) & (y == parity))
                def _():
                    here = own_ref if parity == direction else other_ref
                    there = blocks[0] if parity == 1 - direction else blocks[1]
                    da_ref[link] = here[1] - there[1]
                    weights(len(in_plane), here[0] - there[0])

        kb_ref[link] = 0.5 * (k_ref[2 * w + upward] + k_ref[2 * w + 3 * upward - 1])

    def add(at, step, planes, links):
        rows = [[] for _ in range(planes + links)]
        da = [da_ref[d, at, :] for d in range(link + links)]
        for q in range(terms):
            part = [da[d] * kb_ref[d, q : q + 1, :] for d in range(link + links)]
            for m in range(planes):
                total = (part[4 * m] + part[4 * m + 1]) + (part[4 * m + 2] + part[4 * m + 3])
                if m == 0:
                    total = total + part[across]
                elif m == 1:
                    total = total - part[across]
                rows[m].append(total)
            for index in range(links):
                rows[planes + index].append(part[link + index])
        used = list(range(planes)) + [len(in_plane) + index for index in range(links)]
        out = product(rows, jnp.concatenate([w_ref[m] for m in used], 1))
        out = out.reshape(terms, step, 2 * modes)
        acc_ref[:, at] = out if first else before_ref[:, at] + out

    if extra:
        size = 2 * modes // n_space
        step = min(GROUP, size)
        for mine in (0, 1):
            for at in half_rows(mine, size, step, n_space):
                add(at, step, 2 if mine else 3, linked - mine)
    else:
        for r in range(0, modes, GROUP):
            add(slice(r, r + GROUP), GROUP, 2, linked)

    if stage > 1:
        return

    def edge(slot, here, there, coeff):
        dz_ref[...] = here[1] - there[1]
        kz_ref[...] = coeff
        both = jnp.concatenate(split(here[0] - there[0]), 0)
        wz_ref[...] = jnp.concatenate([both, both], 1)

    slot = edges(stage, (0, 1), 0, n_term, n_space, k_ref, blocks, halo_ref, edge, skip=True)

    @pl.when(slot > 0)
    def _():
        for r in range(0, modes, GROUP):
            dz = dz_ref[r : r + GROUP, :]
            rows = [[dz * kz_ref[q : q + 1, :] for q in range(terms)]]
            out = product(rows, wz_ref[...])
            acc_ref[:, r : r + GROUP] += out.reshape(terms, GROUP, 2 * modes)


def half_rows(mine, size, step, n_space):
    side = lax.axis_index("space") // 2 % 2
    side = side if mine else 1 - side
    return [
        pl.ds(pl.multiple_of((2 * index + side) * size + r, step), step)
        for index in range(n_space // 4)
        for r in range(0, size, step)
    ]


def product(rows, weights):
    left = []
    for part in rows:
        left += split(jnp.concatenate(part, 0))
    return lax.dot_general(jnp.concatenate(left, 1), weights, NT, preferred_element_type=F32)


def edges(stage, sides, slot, n_term, n_space, k_ref, blocks, halo_ref, edge, skip=False, fixed=False):
    pairs = n_term // 2
    modes = blocks[0].shape[1]
    term_at, space_at = lax.axis_index("term"), lax.axis_index("space")
    z, y = term_at // 2, term_at % 2
    w = z ^ stage
    far = stage >= pairs // 2
    is_low = term_at < n_term // 2
    for upward in (0, 1):
        near_w = w + 1 if upward else w - 1
        inside = (near_w >= 0) & (near_w < pairs) & (near_w ^ z < stage)
        for parity in (0, 1):
            side = 0 if parity == upward else 1
            if side not in sides:
                continue
            here = blocks[2 * stage + side]
            mine = y == parity
            if not skip:
                for j in range(stage):
                    @pl.when(inside & mine & (near_w ^ z == j))
                    def _(slot=slot):
                        plane = 2 * w + upward
                        beyond = plane + (1 if upward else -1)
                        edge(slot, here, blocks[2 * j + 1 - side], 0.5 * (k_ref[plane] + k_ref[beyond]))

                slot = slot if fixed else slot + jnp.where(inside & mine, 1, 0)
            used = mine & (w == (pairs - 1 if upward else 0))
            plane = n_term - 1 if upward else 0
            edge_space = space_at == (n_space - 1 if upward else 0)
            if far:
                used = used & (is_low if upward else jnp.logical_not(is_low))
            else:
                used = used & (jnp.logical_not(is_low) if upward else is_low) & edge_space

            @pl.when(used)
            def _(slot=slot):
                if far:
                    came = jnp.where(edge_space, 0.0, halo_ref[...])
                    halo = (came[:modes], came[modes : 2 * modes])
                    edge(slot, here, halo, 0.5 * (k_ref[plane] + came[2 * modes :]))
                else:
                    edge(slot, here, (0.0, 0.0), 0.5 * k_ref[plane])

            slot = slot if fixed else slot + jnp.where(used, 1, 0)
    return slot


def last_kernel(n_term, n_space, mine, *refs):
    pairs = n_term // 2
    k_ref, blocks, rest = refs[0], refs[1 : 1 + n_term], refs[1 + n_term :]
    halo_ref, before_ref, keep_ref, send_ref, acc_ref, da_ref, kb_ref, w_ref = rest
    modes, cells = blocks[0].shape[1:]
    terms = k_ref.shape[1]
    term_at, space_at = lax.axis_index("term"), lax.axis_index("space")
    z, y = term_at // 2, term_at % 2
    w = z ^ (pairs - 1)
    column_ref, other_ref = blocks[-2], blocks[-1]

    def weights(slot, values):
        both = jnp.concatenate(split(values), 0)
        w_ref[slot] = jnp.concatenate([both, both], 1)

    in_plane = [(other_ref, 2 * w + 1 - y)]
    if mine:
        in_plane.append((column_ref, 2 * w + y))
    planes = len(in_plane)
    for m, (ref, plane) in enumerate(in_plane):
        a, k = ref[1], k_ref[plane]
        for d, offset in enumerate(OFFSETS):
            da_ref[4 * m + d] = a - shifted(a, offset)
            kb_ref[4 * m + d] = 0.5 * (k + shifted(k, offset))
        weights(m, ref[0])
    across = 4 * planes
    da_ref[across] = other_ref[1] - column_ref[1]
    kb_ref[across] = 0.5 * (k_ref[2 * w] + k_ref[2 * w + 1])
    links = [across + 1]
    if mine:
        links.append(across + 2)
    else:
        weights(planes + 1, other_ref[0] - column_ref[0])

    def edge(slot, here, there, coeff):
        da_ref[links[slot]] = here[1] - there[1]
        kb_ref[links[slot]] = coeff
        weights(planes + slot, here[0] - there[0])

    for slot in range(len(links)):
        edges(pairs - 1, (1 - slot,), slot, n_term, n_space, k_ref, blocks, halo_ref, edge, fixed=True)

    size = 2 * modes // n_space
    width = modes // n_space
    step = min(GROUP, size)
    for index, at in enumerate(half_rows(mine, size, step, n_space)):
        da = [da_ref[d, at, :] for d in range(links[-1] + 1)]
        rows = [[] for _ in range(planes + 2)]
        for q in range(terms):
            part = [da[d] * kb_ref[d, q : q + 1, :] for d in range(links[-1] + 1)]
            for m in range(planes):
                total = (part[4 * m] + part[4 * m + 1]) + (part[4 * m + 2] + part[4 * m + 3])
                if mine:
                    total = total - part[across] if m else total + part[across]
                rows[m].append(total)
            for slot, d in enumerate(links if mine else links + [across]):
                rows[planes + slot].append(part[d])
        weight = jnp.concatenate([w_ref[m] for m in range(planes + 2)], 1)
        out = product(rows, weight).reshape(terms, step, 2 * modes)
        acc_ref[:, index * step : (index + 1) * step] = before_ref[:, at] + out

    core = space_at % 2
    flat_ref = acc_ref.reshape(terms * (modes // 2), 2 * modes)
    lane = lax.broadcasted_iota(jnp.int32, (terms, 2 * modes), 1)
    for index in range(n_space // 4):
        for j in range(width // 2):
            packed = []
            for at in (index * size + 2 * j, index * size + width + 2 * j):
                even = flat_ref[pl.ds(at, terms, stride=modes // 2), :]
                odd = flat_ref[pl.ds(at + 1, terms, stride=modes // 2), :]
                even = even + pltpu.roll(even, modes, 1)
                odd = odd + pltpu.roll(odd, modes, 1)
                packed.append(jnp.where(lane < modes, even, odd))
            to = slice(2 * modes * j, 2 * modes * (j + 1))
            keep_ref[index, :, to] = jnp.where(core == 0, packed[0], packed[1])
            send_ref[index, :, to] = jnp.where(core == 0, packed[1], packed[0])


def call(kernel, operands, out_shape, scratch, flops=1 << 29):
    whole = pl.BlockSpec(memory_space=pltpu.VMEM)
    return pl.pallas_call(
        kernel,
        out_shape=out_shape,
        in_specs=[whole] * len(operands),
        out_specs=jax.tree.map(lambda _: whole, out_shape),
        scratch_shapes=scratch,
        compiler_params=pltpu.CompilerParams(vmem_limit_bytes=40 << 20),
        cost_estimate=pl.CostEstimate(flops=flops, bytes_accessed=flops >> 7, transcendentals=0),
    )(*operands)


def run_pair(stage, n_term, n_space, coeffs, blocks, halo, before):
    modes, cells = blocks[0].shape[1:]
    terms = coeffs.shape[1]
    extra = len(blocks) - 2 * stage - 2
    operands = [coeffs] + list(blocks)
    if halo is not None:
        operands.append(halo)
    if before is not None:
        operands.append(before)
    kernel = functools.partial(pair_kernel, stage, n_term, n_space, before is None, extra)
    scratch = [
        pltpu.VMEM((16, modes, cells), F32),
        pltpu.VMEM((16, terms, cells), F32),
        pltpu.VMEM((6, 2 * modes, 2 * cells), BF16),
        pltpu.VMEM((modes, cells), F32),
        pltpu.VMEM((terms, cells), F32),
        pltpu.VMEM((2 * modes, 2 * cells), BF16),
    ]
    shape = jax.ShapeDtypeStruct((terms, modes, 2 * modes), F32)
    return call(kernel, operands, shape, scratch)


def run_last(mine, n_term, n_space, coeffs, blocks, halo, before):
    modes, cells = blocks[0].shape[1:]
    terms = coeffs.shape[1]
    scratch = [
        pltpu.VMEM((terms, modes // 2, 2 * modes), F32),
        pltpu.VMEM((11, modes, cells), F32),
        pltpu.VMEM((11, terms, cells), F32),
        pltpu.VMEM((4, 2 * modes, 2 * cells), BF16),
    ]
    shape = jax.ShapeDtypeStruct((n_space // 4, terms, modes * modes // n_space), F32)
    kernel = functools.partial(last_kernel, n_term, n_space, mine)
    return call(kernel, [coeffs] + list(blocks) + [halo, before], [shape, shape], scratch, 0 if mine else 1 << 29)


def exchange(values, axis, apart):
    count = lax.axis_size(axis)
    return lax.ppermute(values, axis, [(i, i ^ apart) for i in range(count)])


def local(right_modes, adjoint_modes, conductivity_terms):
    n_term, n_space = lax.axis_size("term"), lax.axis_size("space")
    term_at, space_at = lax.axis_index("term"), lax.axis_index("space")
    pairs = n_term // 2
    z, y = term_at // 2, term_at % 2
    modes, cells = right_modes.shape[1:]
    terms = conductivity_terms.shape[1]

    def after(x, *deps):
        return lax.optimization_barrier((x,) + deps)[0]

    def go(stage, before, halo=None):
        seen = blocks[: 2 * stage + 2]
        if stage == pairs - 2:
            seen = seen + [blocks[-2]]
        return run_pair(stage, n_term, n_space, conductivity_terms, seen, halo, before)

    which = lax.broadcasted_iota(jnp.int32, (2, 1, 1), 0)
    own = jnp.where(which == 0, right_modes, adjoint_modes)
    half = pairs // 2
    column = {}
    column[half] = exchange(own, "term", 2 * half)
    for stage in range(1, half):
        column[stage] = exchange(own, "term", 2 * stage)
        column[half + stage] = exchange(column[half], "term", 2 * stage)
    blocks = [own, exchange(own, "term", 1)]
    for stage in range(1, half):
        blocks += [column[stage], exchange(column[stage], "term", 1)]
    ahead = [column[half], exchange(column[half], "term", 1)]
    value = go(0, None)
    first_value = value
    blocks = blocks[:2] + [after(x, value) for x in blocks[2:]]
    for stage in range(1, half):
        value = go(stage, value)
    for stage in range(half + 1, pairs):
        came = after(column[stage], value)
        ahead += [came, exchange(came, "term", 1)]
    blocks += ahead

    is_low = term_at < n_term // 2
    wanted = jnp.where(is_low, z, (pairs - 1) ^ z)
    takes_own = (y == 0) == is_low
    rim = after(blocks[0], first_value)
    for j in range(pairs // 2):
        block = jnp.where(takes_own, blocks[2 * j], blocks[2 * j + 1])
        rim = block if j == 0 else jnp.where(wanted == j, block, rim)
    rim_coeff = jnp.where(is_low, conductivity_terms[0], conductivity_terms[-1])
    rim = jnp.concatenate([rim.reshape(2 * modes, cells), rim_coeff], 0)
    route = []
    for s in range(n_space):
        for t in range(n_term):
            low, high = s * n_term + t, (s + 1) % n_space * n_term + t
            route.append((high, low) if t < n_term // 2 else (low, high))
    halo = lax.ppermute(rim, ("space", "term"), route)

    for stage in range(half, pairs - 1):
        value = go(stage, value, halo)
    arguments = (n_term, n_space, conductivity_terms, blocks, halo, value)
    keep, send = run_last(False, *arguments)
    leaving = keep + exchange(send, "space", 1)
    away = exchange(leaving, "space", 2)
    value = after(value, leaving)
    keep, send = run_last(True, n_term, n_space, conductivity_terms, blocks, halo, value)
    middle = terms // 2
    came = [exchange(send[:, :middle], "space", 1), exchange(send[:, middle:], "space", 1)]
    total = keep + jnp.concatenate(came, 1) + away
    apart = 4
    while apart < n_space:
        bit = space_at // apart % 2
        halves = total.reshape((total.shape[0] // 2, 2) + total.shape[1:])
        send = lax.dynamic_index_in_dim(halves, 1 - bit, 1, keepdims=False)
        keep = lax.dynamic_index_in_dim(halves, bit, 1, keepdims=False)
        total = keep + exchange(send, "space", apart)
        apart *= 2
    return total[0]


def solution(mesh):
    placed = (
        P(("space", "term"), None, None),
        P(("space", "term"), None, None),
        P("space", "term", None),
    )
    return jax.shard_map(
        local, mesh=mesh, in_specs=placed, out_specs=P("term", "space"), check_vma=False
    )
```

```python
import functools

import jax
import jax.numpy as jnp
from jax import lax
from jax.experimental import pallas as pl
from jax.experimental.pallas import tpu as pltpu
from jax.sharding import PartitionSpec as P

GY = 32
GROUP = 16
OFFSETS = (GY, -GY, 1, -1)
NT = (((1,), (1,)), ((), ()))
F32 = jnp.float32
BF16 = jnp.bfloat16


def shifted(values, offset):
    width = values.shape[-1]
    lane = lax.broadcasted_iota(jnp.int32, values.shape, values.ndim - 1)
    moved = pltpu.roll(values, (-offset) % width, values.ndim - 1)
    if offset == GY:
        keep = lane < width - GY
    elif offset == -GY:
        keep = lane >= GY
    elif offset == 1:
        keep = lane % GY != GY - 1
    else:
        keep = lane % GY != 0
    return jnp.where(keep, moved, 0.0)


def split(values):
    high = values.astype(BF16)
    return high, (values - high.astype(F32)).astype(BF16)


def pair_kernel(stage, n_term, n_space, first, extra, *refs):
    pairs = n_term // 2
    far = stage >= pairs // 2
    k_ref = refs[0]
    count = 2 * stage + 2 + extra
    blocks = refs[1 : 1 + count]
    rest = list(refs[1 + count :])
    halo_ref = rest.pop(0) if far else None
    before_ref = None if first else rest.pop(0)
    acc_ref, da_ref, kb_ref, w_ref, dz_ref, kz_ref, wz_ref = rest
    modes, cells = blocks[0].shape[1:]
    terms = k_ref.shape[1]
    term_at = lax.axis_index("term")
    z, y = term_at // 2, term_at % 2
    w = z ^ stage
    own_ref, other_ref = blocks[2 * stage], blocks[2 * stage + 1]
    linked = 1 if stage == 1 else 0 if stage == 0 else 1 + extra if pairs == 4 else 2 + extra

    def weights(slot, values):
        both = jnp.concatenate(split(values), 0)
        w_ref[slot] = jnp.concatenate([both, both], 1)

    in_plane = [(own_ref, 2 * w + y), (other_ref, 2 * w + 1 - y)]
    if extra:
        in_plane.append((blocks[-1], 2 * (z ^ (pairs - 1)) + y))
    for m, (ref, plane) in enumerate(in_plane):
        a, k = ref[1], k_ref[plane]
        for d, offset in enumerate(OFFSETS):
            da_ref[4 * m + d] = a - shifted(a, offset)
            kb_ref[4 * m + d] = 0.5 * (k + shifted(k, offset))
        weights(m, ref[0])
    across = 4 * len(in_plane)
    da_ref[across] = own_ref[1] - other_ref[1]
    kb_ref[across] = 0.5 * (k_ref[2 * w + y] + k_ref[2 * w + 1 - y])
    link = across + 1
    if stage > 1:
        def edge(slot, here, there, coeff):
            da_ref[link + slot] = here[1] - there[1]
            kb_ref[link + slot] = coeff
            both = jnp.concatenate(split(here[0] - there[0]), 0)
            w_ref[len(in_plane) + slot] = jnp.concatenate([both, both], 1)

        slot = edges(stage, (0, 1), 0, n_term, n_space, k_ref, blocks, halo_ref, edge)
        if extra:
            edges(pairs - 1, (0,), linked - 1, n_term, n_space, k_ref, blocks, halo_ref, edge, fixed=True)
        for index in range(linked - extra):
            @pl.when(slot <= index)
            def _():
                da_ref[link + index] = jnp.zeros((modes, cells), F32)
                kb_ref[link + index] = jnp.zeros((terms, cells), F32)
                w_ref[len(in_plane) + index] = jnp.zeros((2 * modes, 2 * cells), BF16)

    if stage == 1:
        upward = jnp.where(w % 2 == 0, 1, 0)
        for direction in (0, 1):
            for parity in (0, 1):
                @pl.when((upward == direction) & (y == parity))
                def _():
                    here = own_ref if parity == direction else other_ref
                    there = blocks[0] if parity == 1 - direction else blocks[1]
                    da_ref[link] = here[1] - there[1]
                    weights(len(in_plane), here[0] - there[0])

        kb_ref[link] = 0.5 * (k_ref[2 * w + upward] + k_ref[2 * w + 3 * upward - 1])

    def add(at, step, planes, links):
        rows = [[] for _ in range(planes + links)]
        da = [da_ref[d, at, :] for d in range(link + links)]
        for q in range(terms):
            part = [da[d] * kb_ref[d, q : q + 1, :] for d in range(link + links)]
            for m in range(planes):
                total = (part[4 * m] + part[4 * m + 1]) + (part[4 * m + 2] + part[4 * m + 3])
                if m == 0:
                    total = total + part[across]
                elif m == 1:
                    total = total - part[across]
                rows[m].append(total)
            for index in range(links):
                rows[planes + index].append(part[link + index])
        used = list(range(planes)) + [len(in_plane) + index for index in range(links)]
        out = product(rows, jnp.concatenate([w_ref[m] for m in used], 1))
        out = out.reshape(terms, step, 2 * modes)
        acc_ref[:, at] = out if first else before_ref[:, at] + out

    if extra:
        size = 2 * modes // n_space
        step = min(GROUP, size)
        for mine in (0, 1):
            for at in half_rows(mine, size, step, n_space):
                add(at, step, 2 if mine else 3, linked - mine)
    else:
        for r in range(0, modes, GROUP):
            add(slice(r, r + GROUP), GROUP, 2, linked)

    if stage > 1:
        return

    def edge(slot, here, there, coeff):
        dz_ref[...] = here[1] - there[1]
        kz_ref[...] = coeff
        both = jnp.concatenate(split(here[0] - there[0]), 0)
        wz_ref[...] = jnp.concatenate([both, both], 1)

    slot = edges(stage, (0, 1), 0, n_term, n_space, k_ref, blocks, halo_ref, edge, skip=True)

    @pl.when(slot > 0)
    def _():
        for r in range(0, modes, GROUP):
            dz = dz_ref[r : r + GROUP, :]
            rows = [[dz * kz_ref[q : q + 1, :] for q in range(terms)]]
            out = product(rows, wz_ref[...])
            acc_ref[:, r : r + GROUP] += out.reshape(terms, GROUP, 2 * modes)


def half_rows(mine, size, step, n_space):
    side = lax.axis_index("space") // 2 % 2
    side = side if mine else 1 - side
    return [
        pl.ds(pl.multiple_of((2 * index + side) * size + r, step), step)
        for index in range(n_space // 4)
        for r in range(0, size, step)
    ]


def product(rows, weights):
    left = []
    for part in rows:
        left += split(jnp.concatenate(part, 0))
    return lax.dot_general(jnp.concatenate(left, 1), weights, NT, preferred_element_type=F32)


def edges(stage, sides, slot, n_term, n_space, k_ref, blocks, halo_ref, edge, skip=False, fixed=False):
    pairs = n_term // 2
    modes = blocks[0].shape[1]
    term_at, space_at = lax.axis_index("term"), lax.axis_index("space")
    z, y = term_at // 2, term_at % 2
    w = z ^ stage
    far = stage >= pairs // 2
    is_low = term_at < n_term // 2
    for upward in (0, 1):
        near_w = w + 1 if upward else w - 1
        inside = (near_w >= 0) & (near_w < pairs) & (near_w ^ z < stage)
        for parity in (0, 1):
            side = 0 if parity == upward else 1
            if side not in sides:
                continue
            here = blocks[2 * stage + side]
            mine = y == parity
            if not skip:
                for j in range(stage):
                    @pl.when(inside & mine & (near_w ^ z == j))
                    def _(slot=slot):
                        plane = 2 * w + upward
                        beyond = plane + (1 if upward else -1)
                        edge(slot, here, blocks[2 * j + 1 - side], 0.5 * (k_ref[plane] + k_ref[beyond]))

                slot = slot if fixed else slot + jnp.where(inside & mine, 1, 0)
            used = mine & (w == (pairs - 1 if upward else 0))
            plane = n_term - 1 if upward else 0
            edge_space = space_at == (n_space - 1 if upward else 0)
            if far:
                used = used & (is_low if upward else jnp.logical_not(is_low))
            else:
                used = used & (jnp.logical_not(is_low) if upward else is_low) & edge_space

            @pl.when(used)
            def _(slot=slot):
                if far:
                    came = jnp.where(edge_space, 0.0, halo_ref[...])
                    halo = (came[:modes], came[modes : 2 * modes])
                    edge(slot, here, halo, 0.5 * (k_ref[plane] + came[2 * modes :]))
                else:
                    edge(slot, here, (0.0, 0.0), 0.5 * k_ref[plane])

            slot = slot if fixed else slot + jnp.where(used, 1, 0)
    return slot


def last_kernel(n_term, n_space, mine, *refs):
    pairs = n_term // 2
    k_ref, blocks, rest = refs[0], refs[1 : 1 + n_term], refs[1 + n_term :]
    halo_ref, before_ref, keep_ref, send_ref, acc_ref, da_ref, kb_ref, w_ref = rest
    modes, cells = blocks[0].shape[1:]
    terms = k_ref.shape[1]
    term_at, space_at = lax.axis_index("term"), lax.axis_index("space")
    z, y = term_at // 2, term_at % 2
    w = z ^ (pairs - 1)
    column_ref, other_ref = blocks[-2], blocks[-1]

    def weights(slot, values):
        both = jnp.concatenate(split(values), 0)
        w_ref[slot] = jnp.concatenate([both, both], 1)

    in_plane = [(other_ref, 2 * w + 1 - y)]
    if mine:
        in_plane.append((column_ref, 2 * w + y))
    planes = len(in_plane)
    for m, (ref, plane) in enumerate(in_plane):
        a, k = ref[1], k_ref[plane]
        for d, offset in enumerate(OFFSETS):
            da_ref[4 * m + d] = a - shifted(a, offset)
            kb_ref[4 * m + d] = 0.5 * (k + shifted(k, offset))
        weights(m, ref[0])
    across = 4 * planes
    da_ref[across] = other_ref[1] - column_ref[1]
    kb_ref[across] = 0.5 * (k_ref[2 * w] + k_ref[2 * w + 1])
    links = [across + 1]
    if mine:
        links.append(across + 2)
    else:
        weights(planes + 1, other_ref[0] - column_ref[0])

    def edge(slot, here, there, coeff):
        da_ref[links[slot]] = here[1] - there[1]
        kb_ref[links[slot]] = coeff
        weights(planes + slot, here[0] - there[0])

    for slot in range(len(links)):
        edges(pairs - 1, (1 - slot,), slot, n_term, n_space, k_ref, blocks, halo_ref, edge, fixed=True)

    size = 2 * modes // n_space
    width = modes // n_space
    step = min(GROUP, size)
    for index, at in enumerate(half_rows(mine, size, step, n_space)):
        da = [da_ref[d, at, :] for d in range(links[-1] + 1)]
        rows = [[] for _ in range(planes + 2)]
        for q in range(terms):
            part = [da[d] * kb_ref[d, q : q + 1, :] for d in range(links[-1] + 1)]
            for m in range(planes):
                total = (part[4 * m] + part[4 * m + 1]) + (part[4 * m + 2] + part[4 * m + 3])
                if mine:
                    total = total - part[across] if m else total + part[across]
                rows[m].append(total)
            for slot, d in enumerate(links if mine else links + [across]):
                rows[planes + slot].append(part[d])
        weight = jnp.concatenate([w_ref[m] for m in range(planes + 2)], 1)
        out = product(rows, weight).reshape(terms, step, 2 * modes)
        acc_ref[:terms, index * step : (index + 1) * step] = before_ref[:, at] + out

    core = space_at % 2
    flat_ref = acc_ref.reshape((terms + 1) * (modes // 2), 2 * modes)
    lane = lax.broadcasted_iota(jnp.int32, (terms, 2 * modes), 1)
    for index in range(n_space // 4):
        for j in range(width // 2):
            packed = []
            for at in (index * size + 2 * j, index * size + width + 2 * j):
                even = flat_ref[pl.ds(at, terms, stride=modes // 2), :]
                odd = flat_ref[pl.ds(at + 1, terms, stride=modes // 2), :]
                even = even + pltpu.roll(even, modes, 1)
                odd = odd + pltpu.roll(odd, modes, 1)
                packed.append(jnp.where(lane < modes, even, odd))
            to = slice(2 * modes * j, 2 * modes * (j + 1))
            keep_ref[index, :, to] = jnp.where(core == 0, packed[0], packed[1])
            send_ref[index, :, to] = jnp.where(core == 0, packed[1], packed[0])


def call(kernel, operands, out_shape, scratch, flops=1 << 29):
    whole = pl.BlockSpec(memory_space=pltpu.VMEM)
    return pl.pallas_call(
        kernel,
        out_shape=out_shape,
        in_specs=[whole] * len(operands),
        out_specs=jax.tree.map(lambda _: whole, out_shape),
        scratch_shapes=scratch,
        compiler_params=pltpu.CompilerParams(vmem_limit_bytes=40 << 20),
        cost_estimate=pl.CostEstimate(flops=flops, bytes_accessed=flops >> 7, transcendentals=0),
    )(*operands)


def run_pair(stage, n_term, n_space, coeffs, blocks, halo, before):
    modes, cells = blocks[0].shape[1:]
    terms = coeffs.shape[1]
    extra = len(blocks) - 2 * stage - 2
    operands = [coeffs] + list(blocks)
    if halo is not None:
        operands.append(halo)
    if before is not None:
        operands.append(before)
    kernel = functools.partial(pair_kernel, stage, n_term, n_space, before is None, extra)
    scratch = [
        pltpu.VMEM((16, modes, cells), F32),
        pltpu.VMEM((16, terms, cells), F32),
        pltpu.VMEM((6, 2 * modes, 2 * cells), BF16),
        pltpu.VMEM((modes, cells), F32),
        pltpu.VMEM((terms, cells), F32),
        pltpu.VMEM((2 * modes, 2 * cells), BF16),
    ]
    shape = jax.ShapeDtypeStruct((terms, modes, 2 * modes), F32)
    return call(kernel, operands, shape, scratch)


def run_last(mine, n_term, n_space, coeffs, blocks, halo, before):
    modes, cells = blocks[0].shape[1:]
    terms = coeffs.shape[1]
    scratch = [
        pltpu.VMEM((terms + 1, modes // 2, 2 * modes), F32),
        pltpu.VMEM((11, modes, cells), F32),
        pltpu.VMEM((11, terms, cells), F32),
        pltpu.VMEM((4, 2 * modes, 2 * cells), BF16),
    ]
    shape = jax.ShapeDtypeStruct((n_space // 4, terms, modes * modes // n_space), F32)
    kernel = functools.partial(last_kernel, n_term, n_space, mine)
    return call(kernel, [coeffs] + list(blocks) + [halo, before], [shape, shape], scratch, 0 if mine else 1 << 29)


def exchange(values, axis, apart):
    count = lax.axis_size(axis)
    return lax.ppermute(values, axis, [(i, i ^ apart) for i in range(count)])


def local(right_modes, adjoint_modes, conductivity_terms):
    n_term, n_space = lax.axis_size("term"), lax.axis_size("space")
    term_at, space_at = lax.axis_index("term"), lax.axis_index("space")
    pairs = n_term // 2
    z, y = term_at // 2, term_at % 2
    modes, cells = right_modes.shape[1:]
    terms = conductivity_terms.shape[1]

    def after(x, *deps):
        return lax.optimization_barrier((x,) + deps)[0]

    def go(stage, before, halo=None):
        seen = blocks[: 2 * stage + 2]
        if stage == pairs - 2:
            seen = seen + [blocks[-2]]
        return run_pair(stage, n_term, n_space, conductivity_terms, seen, halo, before)

    which = lax.broadcasted_iota(jnp.int32, (2, 1, 1), 0)
    own = jnp.where(which == 0, right_modes, adjoint_modes)
    half = pairs // 2
    column = {}
    column[half] = exchange(own, "term", 2 * half)
    for stage in range(1, half):
        column[stage] = exchange(own, "term", 2 * stage)
        column[half + stage] = exchange(column[half], "term", 2 * stage)
    blocks = [own, exchange(own, "term", 1)]
    for stage in range(1, half):
        blocks += [column[stage], exchange(column[stage], "term", 1)]
    ahead = [column[half], exchange(column[half], "term", 1)]
    value = go(0, None)
    first_value = value
    blocks = blocks[:2] + [after(x, value) for x in blocks[2:]]
    for stage in range(1, half):
        value = go(stage, value)
    for stage in range(half + 1, pairs):
        came = after(column[stage], value)
        ahead += [came, exchange(came, "term", 1)]
    blocks += ahead

    is_low = term_at < n_term // 2
    wanted = jnp.where(is_low, z, (pairs - 1) ^ z)
    takes_own = (y == 0) == is_low
    rim = after(blocks[0], first_value)
    for j in range(pairs // 2):
        block = jnp.where(takes_own, blocks[2 * j], blocks[2 * j + 1])
        rim = block if j == 0 else jnp.where(wanted == j, block, rim)
    rim_coeff = jnp.where(is_low, conductivity_terms[0], conductivity_terms[-1])
    rim = jnp.concatenate([rim.reshape(2 * modes, cells), rim_coeff], 0)
    route = []
    for s in range(n_space):
        for t in range(n_term):
            low, high = s * n_term + t, (s + 1) % n_space * n_term + t
            route.append((high, low) if t < n_term // 2 else (low, high))
    halo = lax.ppermute(rim, ("space", "term"), route)

    for stage in range(half, pairs - 1):
        value = go(stage, value, halo)
    arguments = (n_term, n_space, conductivity_terms, blocks, halo, value)
    keep, send = run_last(False, *arguments)
    leaving = keep + exchange(send, "space", 1)
    away = exchange(leaving, "space", 2)
    value = after(value, leaving)
    keep, send = run_last(True, n_term, n_space, conductivity_terms, blocks, halo, value)
    middle = terms // 2
    came = [exchange(send[:, :middle], "space", 1), exchange(send[:, middle:], "space", 1)]
    total = keep + jnp.concatenate(came, 1) + away
    apart = 4
    while apart < n_space:
        bit = space_at // apart % 2
        halves = total.reshape((total.shape[0] // 2, 2) + total.shape[1:])
        send = lax.dynamic_index_in_dim(halves, 1 - bit, 1, keepdims=False)
        keep = lax.dynamic_index_in_dim(halves, bit, 1, keepdims=False)
        total = keep + exchange(send, "space", apart)
        apart *= 2
    return total[0]


def solution(mesh):
    placed = (
        P(("space", "term"), None, None),
        P(("space", "term"), None, None),
        P("space", "term", None),
    )
    return jax.shard_map(
        local, mesh=mesh, in_specs=placed, out_specs=P("term", "space"), check_vma=False
    )
```

```python
import functools

import jax
import jax.numpy as jnp
from jax import lax
from jax.experimental import pallas as pl
from jax.experimental.pallas import tpu as pltpu
from jax.sharding import PartitionSpec as P

GY = 32
GROUP = 16
OFFSETS = (GY, -GY, 1, -1)
NT = (((1,), (1,)), ((), ()))
F32 = jnp.float32
BF16 = jnp.bfloat16


def shifted(values, offset):
    width = values.shape[-1]
    lane = lax.broadcasted_iota(jnp.int32, values.shape, values.ndim - 1)
    moved = pltpu.roll(values, (-offset) % width, values.ndim - 1)
    if offset == GY:
        keep = lane < width - GY
    elif offset == -GY:
        keep = lane >= GY
    elif offset == 1:
        keep = lane % GY != GY - 1
    else:
        keep = lane % GY != 0
    return jnp.where(keep, moved, 0.0)


def split(values):
    high = values.astype(BF16)
    return high, (values - high.astype(F32)).astype(BF16)


def pair_kernel(stage, n_term, n_space, first, extra, *refs):
    pairs = n_term // 2
    far = stage >= pairs // 2
    k_ref = refs[0]
    count = 2 * stage + 2 + extra
    blocks = refs[1 : 1 + count]
    rest = list(refs[1 + count :])
    halo_ref = rest.pop(0) if far else None
    before_ref = None if first else rest.pop(0)
    acc_ref, da_ref, kb_ref, w_ref, dz_ref, kz_ref, wz_ref = rest
    modes, cells = blocks[0].shape[1:]
    terms = k_ref.shape[1]
    term_at = lax.axis_index("term")
    z, y = term_at // 2, term_at % 2
    w = z ^ stage
    own_ref, other_ref = blocks[2 * stage], blocks[2 * stage + 1]
    linked = 1 if stage == 1 else 0 if stage == 0 else 1 + extra if pairs == 4 else 2 + extra

    def weights(slot, values):
        both = jnp.concatenate(split(values), 0)
        w_ref[slot] = jnp.concatenate([both, both], 1)

    in_plane = [(own_ref, 2 * w + y), (other_ref, 2 * w + 1 - y)]
    if extra:
        in_plane.append((blocks[-1], 2 * (z ^ (pairs - 1)) + y))
    for m, (ref, plane) in enumerate(in_plane):
        k = k_ref[plane]
        size = 2 * modes // n_space
        for at in half_rows(0, size, size, n_space) if m == 2 else [slice(0, modes)]:
            a = ref[1][at] if m < 2 else ref[1, at, :]
            for d, offset in enumerate(OFFSETS):
                da_ref[4 * m + d, at, :] = a - shifted(a, offset)
        for d, offset in enumerate(OFFSETS):
            kb_ref[4 * m + d] = 0.5 * (k + shifted(k, offset))
        weights(m, ref[0])
    across = 4 * len(in_plane)
    da_ref[across] = own_ref[1] - other_ref[1]
    kb_ref[across] = 0.5 * (k_ref[2 * w + y] + k_ref[2 * w + 1 - y])
    link = across + 1
    if stage > 1:
        def edge(slot, here, there, coeff):
            da_ref[link + slot] = here[1] - there[1]
            kb_ref[link + slot] = coeff
            both = jnp.concatenate(split(here[0] - there[0]), 0)
            w_ref[len(in_plane) + slot] = jnp.concatenate([both, both], 1)

        slot = edges(stage, (0, 1), 0, n_term, n_space, k_ref, blocks, halo_ref, edge)
        if extra:
            edges(pairs - 1, (0,), linked - 1, n_term, n_space, k_ref, blocks, halo_ref, edge, fixed=True)
        for index in range(linked - extra):
            @pl.when(slot <= index)
            def _():
                da_ref[link + index] = jnp.zeros((modes, cells), F32)
                kb_ref[link + index] = jnp.zeros((terms, cells), F32)
                w_ref[len(in_plane) + index] = jnp.zeros((2 * modes, 2 * cells), BF16)

    if stage == 1:
        upward = jnp.where(w % 2 == 0, 1, 0)
        for direction in (0, 1):
            for parity in (0, 1):
                @pl.when((upward == direction) & (y == parity))
                def _():
                    here = own_ref if parity == direction else other_ref
                    there = blocks[0] if parity == 1 - direction else blocks[1]
                    da_ref[link] = here[1] - there[1]
                    weights(len(in_plane), here[0] - there[0])

        kb_ref[link] = 0.5 * (k_ref[2 * w + upward] + k_ref[2 * w + 3 * upward - 1])

    def add(at, step, planes, links):
        rows = [[] for _ in range(planes + links)]
        da = [da_ref[d, at, :] for d in range(link + links)]
        for q in range(terms):
            part = [da[d] * kb_ref[d, q : q + 1, :] for d in range(link + links)]
            for m in range(planes):
                total = (part[4 * m] + part[4 * m + 1]) + (part[4 * m + 2] + part[4 * m + 3])
                if m == 0:
                    total = total + part[across]
                elif m == 1:
                    total = total - part[across]
                rows[m].append(total)
            for index in range(links):
                rows[planes + index].append(part[link + index])
        used = list(range(planes)) + [len(in_plane) + index for index in range(links)]
        out = product(rows, jnp.concatenate([w_ref[m] for m in used], 1))
        out = out.reshape(terms, step, 2 * modes)
        acc_ref[:, at] = out if first else before_ref[:, at] + out

    if extra:
        size = 2 * modes // n_space
        step = min(GROUP, size)
        for mine in (0, 1):
            for at in half_rows(mine, size, step, n_space):
                add(at, step, 2 if mine else 3, linked - mine)
    else:
        for r in range(0, modes, GROUP):
            add(slice(r, r + GROUP), GROUP, 2, linked)

    if stage > 1:
        return

    def edge(slot, here, there, coeff):
        dz_ref[...] = here[1] - there[1]
        kz_ref[...] = coeff
        both = jnp.concatenate(split(here[0] - there[0]), 0)
        wz_ref[...] = jnp.concatenate([both, both], 1)

    slot = edges(stage, (0, 1), 0, n_term, n_space, k_ref, blocks, halo_ref, edge, skip=True)

    @pl.when(slot > 0)
    def _():
        for r in range(0, modes, GROUP):
            dz = dz_ref[r : r + GROUP, :]
            rows = [[dz * kz_ref[q : q + 1, :] for q in range(terms)]]
            out = product(rows, wz_ref[...])
            acc_ref[:, r : r + GROUP] += out.reshape(terms, GROUP, 2 * modes)


def half_rows(mine, size, step, n_space):
    side = lax.axis_index("space") // 2 % 2
    side = side if mine else 1 - side
    return [
        pl.ds(pl.multiple_of((2 * index + side) * size + r, step), step)
        for index in range(n_space // 4)
        for r in range(0, size, step)
    ]


def product(rows, weights):
    left = []
    for part in rows:
        left += split(jnp.concatenate(part, 0))
    return lax.dot_general(jnp.concatenate(left, 1), weights, NT, preferred_element_type=F32)


def edges(stage, sides, slot, n_term, n_space, k_ref, blocks, halo_ref, edge, skip=False, fixed=False):
    pairs = n_term // 2
    modes = blocks[0].shape[1]
    term_at, space_at = lax.axis_index("term"), lax.axis_index("space")
    z, y = term_at // 2, term_at % 2
    w = z ^ stage
    far = stage >= pairs // 2
    is_low = term_at < n_term // 2
    for upward in (0, 1):
        near_w = w + 1 if upward else w - 1
        inside = (near_w >= 0) & (near_w < pairs) & (near_w ^ z < stage)
        for parity in (0, 1):
            side = 0 if parity == upward else 1
            if side not in sides:
                continue
            here = blocks[2 * stage + side]
            mine = y == parity
            if not skip:
                for j in range(stage):
                    @pl.when(inside & mine & (near_w ^ z == j))
                    def _(slot=slot):
                        plane = 2 * w + upward
                        beyond = plane + (1 if upward else -1)
                        edge(slot, here, blocks[2 * j + 1 - side], 0.5 * (k_ref[plane] + k_ref[beyond]))

                slot = slot if fixed else slot + jnp.where(inside & mine, 1, 0)
            used = mine & (w == (pairs - 1 if upward else 0))
            plane = n_term - 1 if upward else 0
            edge_space = space_at == (n_space - 1 if upward else 0)
            if far:
                used = used & (is_low if upward else jnp.logical_not(is_low))
            else:
                used = used & (jnp.logical_not(is_low) if upward else is_low) & edge_space

            @pl.when(used)
            def _(slot=slot):
                if far:
                    came = jnp.where(edge_space, 0.0, halo_ref[...])
                    halo = (came[:modes], came[modes : 2 * modes])
                    edge(slot, here, halo, 0.5 * (k_ref[plane] + came[2 * modes :]))
                else:
                    edge(slot, here, (0.0, 0.0), 0.5 * k_ref[plane])

            slot = slot if fixed else slot + jnp.where(used, 1, 0)
    return slot


def last_kernel(n_term, n_space, mine, *refs):
    pairs = n_term // 2
    k_ref, blocks, rest = refs[0], refs[1 : 1 + n_term], refs[1 + n_term :]
    halo_ref, before_ref, keep_ref, send_ref, acc_ref, da_ref, kb_ref, w_ref = rest
    modes, cells = blocks[0].shape[1:]
    terms = k_ref.shape[1]
    term_at, space_at = lax.axis_index("term"), lax.axis_index("space")
    z, y = term_at // 2, term_at % 2
    w = z ^ (pairs - 1)
    column_ref, other_ref = blocks[-2], blocks[-1]

    def weights(slot, values):
        both = jnp.concatenate(split(values), 0)
        w_ref[slot] = jnp.concatenate([both, both], 1)

    in_plane = [(other_ref, 2 * w + 1 - y)]
    if mine:
        in_plane.append((column_ref, 2 * w + y))
    planes = len(in_plane)
    for m, (ref, plane) in enumerate(in_plane):
        k = k_ref[plane]
        for at in half_rows(mine, 2 * modes // n_space, 2 * modes // n_space, n_space):
            a = ref[1, at, :]
            for d, offset in enumerate(OFFSETS):
                da_ref[4 * m + d, at, :] = a - shifted(a, offset)
        for d, offset in enumerate(OFFSETS):
            kb_ref[4 * m + d] = 0.5 * (k + shifted(k, offset))
        weights(m, ref[0])
    across = 4 * planes
    da_ref[across] = other_ref[1] - column_ref[1]
    kb_ref[across] = 0.5 * (k_ref[2 * w] + k_ref[2 * w + 1])
    links = [across + 1]
    if mine:
        links.append(across + 2)
    else:
        weights(planes + 1, other_ref[0] - column_ref[0])

    def edge(slot, here, there, coeff):
        da_ref[links[slot]] = here[1] - there[1]
        kb_ref[links[slot]] = coeff
        weights(planes + slot, here[0] - there[0])

    for slot in range(len(links)):
        edges(pairs - 1, (1 - slot,), slot, n_term, n_space, k_ref, blocks, halo_ref, edge, fixed=True)

    size = 2 * modes // n_space
    width = modes // n_space
    step = min(GROUP, size)
    for index, at in enumerate(half_rows(mine, size, step, n_space)):
        da = [da_ref[d, at, :] for d in range(links[-1] + 1)]
        rows = [[] for _ in range(planes + 2)]
        for q in range(terms):
            part = [da[d] * kb_ref[d, q : q + 1, :] for d in range(links[-1] + 1)]
            for m in range(planes):
                total = (part[4 * m] + part[4 * m + 1]) + (part[4 * m + 2] + part[4 * m + 3])
                if mine:
                    total = total - part[across] if m else total + part[across]
                rows[m].append(total)
            for slot, d in enumerate(links if mine else links + [across]):
                rows[planes + slot].append(part[d])
        weight = jnp.concatenate([w_ref[m] for m in range(planes + 2)], 1)
        out = product(rows, weight).reshape(terms, step, 2 * modes)
        acc_ref[:terms, index * step : (index + 1) * step] = before_ref[:, at] + out

    core = space_at % 2
    flat_ref = acc_ref.reshape((terms + 1) * (modes // 2), 2 * modes)
    lane = lax.broadcasted_iota(jnp.int32, (terms, 2 * modes), 1)
    for index in range(n_space // 4):
        for j in range(width // 2):
            packed = []
            for at in (index * size + 2 * j, index * size + width + 2 * j):
                even = flat_ref[pl.ds(at, terms, stride=modes // 2), :]
                odd = flat_ref[pl.ds(at + 1, terms, stride=modes // 2), :]
                even = even + pltpu.roll(even, modes, 1)
                odd = odd + pltpu.roll(odd, modes, 1)
                packed.append(jnp.where(lane < modes, even, odd))
            to = slice(2 * modes * j, 2 * modes * (j + 1))
            keep_ref[index, :, to] = jnp.where(core == 0, packed[0], packed[1])
            send_ref[index, :, to] = jnp.where(core == 0, packed[1], packed[0])


def call(kernel, operands, out_shape, scratch, flops=1 << 29):
    whole = pl.BlockSpec(memory_space=pltpu.VMEM)
    return pl.pallas_call(
        kernel,
        out_shape=out_shape,
        in_specs=[whole] * len(operands),
        out_specs=jax.tree.map(lambda _: whole, out_shape),
        scratch_shapes=scratch,
        compiler_params=pltpu.CompilerParams(vmem_limit_bytes=40 << 20),
        cost_estimate=pl.CostEstimate(flops=flops, bytes_accessed=flops >> 7, transcendentals=0),
    )(*operands)


def run_pair(stage, n_term, n_space, coeffs, blocks, halo, before):
    modes, cells = blocks[0].shape[1:]
    terms = coeffs.shape[1]
    extra = len(blocks) - 2 * stage - 2
    operands = [coeffs] + list(blocks)
    if halo is not None:
        operands.append(halo)
    if before is not None:
        operands.append(before)
    kernel = functools.partial(pair_kernel, stage, n_term, n_space, before is None, extra)
    scratch = [
        pltpu.VMEM((16, modes, cells), F32),
        pltpu.VMEM((16, terms, cells), F32),
        pltpu.VMEM((6, 2 * modes, 2 * cells), BF16),
        pltpu.VMEM((modes, cells), F32),
        pltpu.VMEM((terms, cells), F32),
        pltpu.VMEM((2 * modes, 2 * cells), BF16),
    ]
    shape = jax.ShapeDtypeStruct((terms, modes, 2 * modes), F32)
    return call(kernel, operands, shape, scratch)


def run_last(mine, n_term, n_space, coeffs, blocks, halo, before):
    modes, cells = blocks[0].shape[1:]
    terms = coeffs.shape[1]
    scratch = [
        pltpu.VMEM((terms + 1, modes // 2, 2 * modes), F32),
        pltpu.VMEM((11, modes, cells), F32),
        pltpu.VMEM((11, terms, cells), F32),
        pltpu.VMEM((4, 2 * modes, 2 * cells), BF16),
    ]
    shape = jax.ShapeDtypeStruct((n_space // 4, terms, modes * modes // n_space), F32)
    kernel = functools.partial(last_kernel, n_term, n_space, mine)
    return call(kernel, [coeffs] + list(blocks) + [halo, before], [shape, shape], scratch, 0 if mine else 1 << 29)


def exchange(values, axis, apart):
    count = lax.axis_size(axis)
    return lax.ppermute(values, axis, [(i, i ^ apart) for i in range(count)])


def local(right_modes, adjoint_modes, conductivity_terms):
    n_term, n_space = lax.axis_size("term"), lax.axis_size("space")
    term_at, space_at = lax.axis_index("term"), lax.axis_index("space")
    pairs = n_term // 2
    z, y = term_at // 2, term_at % 2
    modes, cells = right_modes.shape[1:]
    terms = conductivity_terms.shape[1]

    def after(x, *deps):
        return lax.optimization_barrier((x,) + deps)[0]

    def go(stage, before, halo=None):
        seen = blocks[: 2 * stage + 2]
        if stage == pairs - 2:
            seen = seen + [blocks[-2]]
        return run_pair(stage, n_term, n_space, conductivity_terms, seen, halo, before)

    which = lax.broadcasted_iota(jnp.int32, (2, 1, 1), 0)
    own = jnp.where(which == 0, right_modes, adjoint_modes)
    half = pairs // 2
    column = {}
    column[half] = exchange(own, "term", 2 * half)
    for stage in range(1, half):
        column[stage] = exchange(own, "term", 2 * stage)
        column[half + stage] = exchange(column[half], "term", 2 * stage)
    blocks = [own, exchange(own, "term", 1)]
    for stage in range(1, half):
        blocks += [column[stage], exchange(column[stage], "term", 1)]
    ahead = [column[half], exchange(column[half], "term", 1)]
    value = go(0, None)
    first_value = value
    blocks = blocks[:2] + [after(x, value) for x in blocks[2:]]
    for stage in range(1, half):
        value = go(stage, value)
    for stage in range(half + 1, pairs):
        came = after(column[stage], value)
        ahead += [came, exchange(came, "term", 1)]
    blocks += ahead

    is_low = term_at < n_term // 2
    wanted = jnp.where(is_low, z, (pairs - 1) ^ z)
    takes_own = (y == 0) == is_low
    rim = after(blocks[0], first_value)
    for j in range(pairs // 2):
        block = jnp.where(takes_own, blocks[2 * j], blocks[2 * j + 1])
        rim = block if j == 0 else jnp.where(wanted == j, block, rim)
    rim_coeff = jnp.where(is_low, conductivity_terms[0], conductivity_terms[-1])
    rim = jnp.concatenate([rim.reshape(2 * modes, cells), rim_coeff], 0)
    route = []
    for s in range(n_space):
        for t in range(n_term):
            low, high = s * n_term + t, (s + 1) % n_space * n_term + t
            route.append((high, low) if t < n_term // 2 else (low, high))
    halo = lax.ppermute(rim, ("space", "term"), route)

    for stage in range(half, pairs - 1):
        value = go(stage, value, halo)
    arguments = (n_term, n_space, conductivity_terms, blocks, halo, value)
    keep, send = run_last(False, *arguments)
    leaving = keep + exchange(send, "space", 1)
    away = exchange(leaving, "space", 2)
    value = after(value, leaving)
    keep, send = run_last(True, n_term, n_space, conductivity_terms, blocks, halo, value)
    middle = terms // 2
    came = [exchange(send[:, :middle], "space", 1), exchange(send[:, middle:], "space", 1)]
    total = keep + jnp.concatenate(came, 1) + away
    apart = 4
    while apart < n_space:
        bit = space_at // apart % 2
        halves = total.reshape((total.shape[0] // 2, 2) + total.shape[1:])
        send = lax.dynamic_index_in_dim(halves, 1 - bit, 1, keepdims=False)
        keep = lax.dynamic_index_in_dim(halves, bit, 1, keepdims=False)
        total = keep + exchange(send, "space", apart)
        apart *= 2
    return total[0]


def solution(mesh):
    placed = (
        P(("space", "term"), None, None),
        P(("space", "term"), None, None),
        P("space", "term", None),
    )
    return jax.shard_map(
        local, mesh=mesh, in_specs=placed, out_specs=P("term", "space"), check_vma=False
    )
```

```python
import functools

import jax
import jax.numpy as jnp
from jax import lax
from jax.experimental import pallas as pl
from jax.experimental.pallas import tpu as pltpu
from jax.sharding import PartitionSpec as P

GY = 32
GROUP = 16
OFFSETS = (GY, -GY, 1, -1)
NT = (((1,), (1,)), ((), ()))
F32 = jnp.float32
BF16 = jnp.bfloat16


def shifted(values, offset):
    width = values.shape[-1]
    lane = lax.broadcasted_iota(jnp.int32, values.shape, values.ndim - 1)
    moved = pltpu.roll(values, (-offset) % width, values.ndim - 1)
    if offset == GY:
        keep = lane < width - GY
    elif offset == -GY:
        keep = lane >= GY
    elif offset == 1:
        keep = lane % GY != GY - 1
    else:
        keep = lane % GY != 0
    return jnp.where(keep, moved, 0.0)


def split(values):
    high = values.astype(BF16)
    return high, (values - high.astype(F32)).astype(BF16)


def pair_kernel(stage, n_term, n_space, first, extra, *refs):
    pairs = n_term // 2
    far = stage >= pairs // 2
    k_ref = refs[0]
    count = 2 * stage + 2 + extra
    blocks = refs[1 : 1 + count]
    rest = list(refs[1 + count :])
    halo_ref = rest.pop(0) if far else None
    before_ref = None if first else rest.pop(0)
    acc_ref, da_ref, kb_ref, w_ref, dz_ref, kz_ref, wz_ref = rest
    modes, cells = blocks[0].shape[1:]
    terms = k_ref.shape[1]
    term_at = lax.axis_index("term")
    z, y = term_at // 2, term_at % 2
    w = z ^ stage
    own_ref, other_ref = blocks[2 * stage], blocks[2 * stage + 1]
    linked = 1 if stage == 1 else 0 if stage == 0 else 1 + extra if pairs == 4 else 2 + extra

    def weights(slot, values):
        w_ref[slot] = jnp.concatenate(split(values), 0)

    in_plane = [(own_ref, 2 * w + y), (other_ref, 2 * w + 1 - y)]
    if extra:
        in_plane.append((blocks[-1], 2 * (z ^ (pairs - 1)) + y))
    for m, (ref, plane) in enumerate(in_plane):
        k = k_ref[plane]
        size = 2 * modes // n_space
        for at in half_rows(0, size, size, n_space) if m == 2 else [slice(0, modes)]:
            a = ref[1][at] if m < 2 else ref[1, at, :]
            for d, offset in enumerate(OFFSETS):
                da_ref[4 * m + d, at, :] = a - shifted(a, offset)
        for d, offset in enumerate(OFFSETS):
            kb_ref[4 * m + d] = 0.5 * (k + shifted(k, offset))
        weights(m, ref[0])
    across = 4 * len(in_plane)
    da_ref[across] = own_ref[1] - other_ref[1]
    kb_ref[across] = 0.5 * (k_ref[2 * w + y] + k_ref[2 * w + 1 - y])
    link = across + 1
    if stage > 1:
        def edge(slot, here, there, coeff):
            da_ref[link + slot] = here[1] - there[1]
            kb_ref[link + slot] = coeff
            w_ref[len(in_plane) + slot] = jnp.concatenate(split(here[0] - there[0]), 0)

        slot = edges(stage, (0, 1), 0, n_term, n_space, k_ref, blocks, halo_ref, edge)
        if extra:
            edges(pairs - 1, (0,), linked - 1, n_term, n_space, k_ref, blocks, halo_ref, edge, fixed=True)
        for index in range(linked - extra):
            @pl.when(slot <= index)
            def _():
                da_ref[link + index] = jnp.zeros((modes, cells), F32)
                kb_ref[link + index] = jnp.zeros((terms, cells), F32)
                w_ref[len(in_plane) + index] = jnp.zeros((2 * modes, cells), BF16)

    if stage == 1:
        upward = jnp.where(w % 2 == 0, 1, 0)
        for direction in (0, 1):
            for parity in (0, 1):
                @pl.when((upward == direction) & (y == parity))
                def _():
                    here = own_ref if parity == direction else other_ref
                    there = blocks[0] if parity == 1 - direction else blocks[1]
                    da_ref[link] = here[1] - there[1]
                    weights(len(in_plane), here[0] - there[0])

        kb_ref[link] = 0.5 * (k_ref[2 * w + upward] + k_ref[2 * w + 3 * upward - 1])

    def add(at, step, planes, links):
        rows = [[] for _ in range(planes + links)]
        da = [da_ref[d, at, :] for d in range(link + links)]
        for q in range(terms):
            part = [da[d] * kb_ref[d, q : q + 1, :] for d in range(link + links)]
            for m in range(planes):
                total = (part[4 * m] + part[4 * m + 1]) + (part[4 * m + 2] + part[4 * m + 3])
                if m == 0:
                    total = total + part[across]
                elif m == 1:
                    total = total - part[across]
                rows[m].append(total)
            for index in range(links):
                rows[planes + index].append(part[link + index])
        used = list(range(planes)) + [len(in_plane) + index for index in range(links)]
        out = product(rows, jnp.concatenate([w_ref[m] for m in used for _ in (0, 1)], 1))
        out = out.reshape(terms, step, 2 * modes)
        acc_ref[:, at] = out if first else before_ref[:, at] + out

    if extra:
        size = 2 * modes // n_space
        step = min(GROUP, size)
        for mine in (0, 1):
            for at in half_rows(mine, size, step, n_space):
                add(at, step, 2 if mine else 3, linked - mine)
    else:
        for r in range(0, modes, GROUP):
            add(slice(r, r + GROUP), GROUP, 2, linked)

    if stage > 1:
        return

    def edge(slot, here, there, coeff):
        dz_ref[...] = here[1] - there[1]
        kz_ref[...] = coeff
        wz_ref[...] = jnp.concatenate(split(here[0] - there[0]), 0)

    slot = edges(stage, (0, 1), 0, n_term, n_space, k_ref, blocks, halo_ref, edge, skip=True)

    @pl.when(slot > 0)
    def _():
        for r in range(0, modes, GROUP):
            dz = dz_ref[r : r + GROUP, :]
            rows = [[dz * kz_ref[q : q + 1, :] for q in range(terms)]]
            out = product(rows, jnp.concatenate([wz_ref[...], wz_ref[...]], 1))
            acc_ref[:, r : r + GROUP] += out.reshape(terms, GROUP, 2 * modes)


def half_rows(mine, size, step, n_space):
    side = lax.axis_index("space") // 2 % 2
    side = side if mine else 1 - side
    return [
        pl.ds(pl.multiple_of((2 * index + side) * size + r, step), step)
        for index in range(n_space // 4)
        for r in range(0, size, step)
    ]


def product(rows, weights):
    left = []
    for part in rows:
        left += split(jnp.concatenate(part, 0))
    return lax.dot_general(jnp.concatenate(left, 1), weights, NT, preferred_element_type=F32)


def edges(stage, sides, slot, n_term, n_space, k_ref, blocks, halo_ref, edge, skip=False, fixed=False):
    pairs = n_term // 2
    modes = blocks[0].shape[1]
    term_at, space_at = lax.axis_index("term"), lax.axis_index("space")
    z, y = term_at // 2, term_at % 2
    w = z ^ stage
    far = stage >= pairs // 2
    is_low = term_at < n_term // 2
    for upward in (0, 1):
        near_w = w + 1 if upward else w - 1
        inside = (near_w >= 0) & (near_w < pairs) & (near_w ^ z < stage)
        for parity in (0, 1):
            side = 0 if parity == upward else 1
            if side not in sides:
                continue
            here = blocks[2 * stage + side]
            mine = y == parity
            if not skip:
                for j in range(stage):
                    @pl.when(inside & mine & (near_w ^ z == j))
                    def _(slot=slot):
                        plane = 2 * w + upward
                        beyond = plane + (1 if upward else -1)
                        edge(slot, here, blocks[2 * j + 1 - side], 0.5 * (k_ref[plane] + k_ref[beyond]))

                slot = slot if fixed else slot + jnp.where(inside & mine, 1, 0)
            used = mine & (w == (pairs - 1 if upward else 0))
            plane = n_term - 1 if upward else 0
            edge_space = space_at == (n_space - 1 if upward else 0)
            if far:
                used = used & (is_low if upward else jnp.logical_not(is_low))
            else:
                used = used & (jnp.logical_not(is_low) if upward else is_low) & edge_space

            @pl.when(used)
            def _(slot=slot):
                if far:
                    came = jnp.where(edge_space, 0.0, halo_ref[...])
                    halo = (came[:modes], came[modes : 2 * modes])
                    edge(slot, here, halo, 0.5 * (k_ref[plane] + came[2 * modes :]))
                else:
                    edge(slot, here, (0.0, 0.0), 0.5 * k_ref[plane])

            slot = slot if fixed else slot + jnp.where(used, 1, 0)
    return slot


def last_kernel(n_term, n_space, mine, *refs):
    pairs = n_term // 2
    k_ref, blocks, rest = refs[0], refs[1 : 1 + n_term], refs[1 + n_term :]
    halo_ref, before_ref, keep_ref, send_ref, acc_ref, da_ref, kb_ref, w_ref = rest
    modes, cells = blocks[0].shape[1:]
    terms = k_ref.shape[1]
    term_at, space_at = lax.axis_index("term"), lax.axis_index("space")
    z, y = term_at // 2, term_at % 2
    w = z ^ (pairs - 1)
    column_ref, other_ref = blocks[-2], blocks[-1]

    def weights(slot, values):
        w_ref[slot] = jnp.concatenate(split(values), 0)

    in_plane = [(other_ref, 2 * w + 1 - y)]
    if mine:
        in_plane.append((column_ref, 2 * w + y))
    planes = len(in_plane)
    for m, (ref, plane) in enumerate(in_plane):
        k = k_ref[plane]
        for at in half_rows(mine, 2 * modes // n_space, 2 * modes // n_space, n_space):
            a = ref[1, at, :]
            for d, offset in enumerate(OFFSETS):
                da_ref[4 * m + d, at, :] = a - shifted(a, offset)
        for d, offset in enumerate(OFFSETS):
            kb_ref[4 * m + d] = 0.5 * (k + shifted(k, offset))
        weights(m, ref[0])
    across = 4 * planes
    da_ref[across] = other_ref[1] - column_ref[1]
    kb_ref[across] = 0.5 * (k_ref[2 * w] + k_ref[2 * w + 1])
    links = [across + 1]
    if mine:
        links.append(across + 2)
    else:
        weights(planes + 1, other_ref[0] - column_ref[0])

    def edge(slot, here, there, coeff):
        da_ref[links[slot]] = here[1] - there[1]
        kb_ref[links[slot]] = coeff
        weights(planes + slot, here[0] - there[0])

    for slot in range(len(links)):
        edges(pairs - 1, (1 - slot,), slot, n_term, n_space, k_ref, blocks, halo_ref, edge, fixed=True)

    size = 2 * modes // n_space
    width = modes // n_space
    step = min(GROUP, size)
    for index, at in enumerate(half_rows(mine, size, step, n_space)):
        da = [da_ref[d, at, :] for d in range(links[-1] + 1)]
        rows = [[] for _ in range(planes + 2)]
        for q in range(terms):
            part = [da[d] * kb_ref[d, q : q + 1, :] for d in range(links[-1] + 1)]
            for m in range(planes):
                total = (part[4 * m] + part[4 * m + 1]) + (part[4 * m + 2] + part[4 * m + 3])
                if mine:
                    total = total - part[across] if m else total + part[across]
                rows[m].append(total)
            for slot, d in enumerate(links if mine else links + [across]):
                rows[planes + slot].append(part[d])
        weight = jnp.concatenate([w_ref[m] for m in range(planes + 2) for _ in (0, 1)], 1)
        out = product(rows, weight).reshape(terms, step, 2 * modes)
        acc_ref[:terms, index * step : (index + 1) * step] = before_ref[:, at] + out

    core = space_at % 2
    flat_ref = acc_ref.reshape((terms + 1) * (modes // 2), 2 * modes)
    lane = lax.broadcasted_iota(jnp.int32, (terms, 2 * modes), 1)
    for index in range(n_space // 4):
        for j in range(width // 2):
            packed = []
            for at in (index * size + 2 * j, index * size + width + 2 * j):
                even = flat_ref[pl.ds(at, terms, stride=modes // 2), :]
                odd = flat_ref[pl.ds(at + 1, terms, stride=modes // 2), :]
                even = even + pltpu.roll(even, modes, 1)
                odd = odd + pltpu.roll(odd, modes, 1)
                packed.append(jnp.where(lane < modes, even, odd))
            to = slice(2 * modes * j, 2 * modes * (j + 1))
            keep_ref[index, :, to] = jnp.where(core == 0, packed[0], packed[1])
            send_ref[index, :, to] = jnp.where(core == 0, packed[1], packed[0])


def call(kernel, operands, out_shape, scratch, flops=1 << 29):
    whole = pl.BlockSpec(memory_space=pltpu.VMEM)
    return pl.pallas_call(
        kernel,
        out_shape=out_shape,
        in_specs=[whole] * len(operands),
        out_specs=jax.tree.map(lambda _: whole, out_shape),
        scratch_shapes=scratch,
        compiler_params=pltpu.CompilerParams(vmem_limit_bytes=40 << 20),
        cost_estimate=pl.CostEstimate(flops=flops, bytes_accessed=flops >> 7, transcendentals=0),
    )(*operands)


def run_pair(stage, n_term, n_space, coeffs, blocks, halo, before):
    modes, cells = blocks[0].shape[1:]
    terms = coeffs.shape[1]
    extra = len(blocks) - 2 * stage - 2
    operands = [coeffs] + list(blocks)
    if halo is not None:
        operands.append(halo)
    if before is not None:
        operands.append(before)
    kernel = functools.partial(pair_kernel, stage, n_term, n_space, before is None, extra)
    scratch = [
        pltpu.VMEM((16, modes, cells), F32),
        pltpu.VMEM((16, terms, cells), F32),
        pltpu.VMEM((6, 2 * modes, cells), BF16),
        pltpu.VMEM((modes, cells), F32),
        pltpu.VMEM((terms, cells), F32),
        pltpu.VMEM((2 * modes, cells), BF16),
    ]
    shape = jax.ShapeDtypeStruct((terms, modes, 2 * modes), F32)
    return call(kernel, operands, shape, scratch)


def run_last(mine, n_term, n_space, coeffs, blocks, halo, before):
    modes, cells = blocks[0].shape[1:]
    terms = coeffs.shape[1]
    scratch = [
        pltpu.VMEM((terms + 1, modes // 2, 2 * modes), F32),
        pltpu.VMEM((11, modes, cells), F32),
        pltpu.VMEM((11, terms, cells), F32),
        pltpu.VMEM((4, 2 * modes, cells), BF16),
    ]
    shape = jax.ShapeDtypeStruct((n_space // 4, terms, modes * modes // n_space), F32)
    kernel = functools.partial(last_kernel, n_term, n_space, mine)
    return call(kernel, [coeffs] + list(blocks) + [halo, before], [shape, shape], scratch, 0 if mine else 1 << 29)


def exchange(values, axis, apart):
    count = lax.axis_size(axis)
    return lax.ppermute(values, axis, [(i, i ^ apart) for i in range(count)])


def local(right_modes, adjoint_modes, conductivity_terms):
    n_term, n_space = lax.axis_size("term"), lax.axis_size("space")
    term_at, space_at = lax.axis_index("term"), lax.axis_index("space")
    pairs = n_term // 2
    z, y = term_at // 2, term_at % 2
    modes, cells = right_modes.shape[1:]
    terms = conductivity_terms.shape[1]

    def after(x, *deps):
        return lax.optimization_barrier((x,) + deps)[0]

    def go(stage, before, halo=None):
        seen = blocks[: 2 * stage + 2]
        if stage == pairs - 2:
            seen = seen + [blocks[-2]]
        return run_pair(stage, n_term, n_space, conductivity_terms, seen, halo, before)

    which = lax.broadcasted_iota(jnp.int32, (2, 1, 1), 0)
    own = jnp.where(which == 0, right_modes, adjoint_modes)
    half = pairs // 2
    column = {}
    column[half] = exchange(own, "term", 2 * half)
    for stage in range(1, half):
        column[stage] = exchange(own, "term", 2 * stage)
        column[half + stage] = exchange(column[half], "term", 2 * stage)
    blocks = [own, exchange(own, "term", 1)]
    for stage in range(1, half):
        blocks += [column[stage], exchange(column[stage], "term", 1)]
    ahead = [column[half], exchange(column[half], "term", 1)]
    value = go(0, None)
    first_value = value
    blocks = blocks[:2] + [after(x, value) for x in blocks[2:]]
    for stage in range(1, half):
        value = go(stage, value)
    for stage in range(half + 1, pairs):
        came = after(column[stage], value)
        ahead += [came, exchange(came, "term", 1)]
    blocks += ahead

    is_low = term_at < n_term // 2
    wanted = jnp.where(is_low, z, (pairs - 1) ^ z)
    takes_own = (y == 0) == is_low
    rim = after(blocks[0], first_value)
    for j in range(pairs // 2):
        block = jnp.where(takes_own, blocks[2 * j], blocks[2 * j + 1])
        rim = block if j == 0 else jnp.where(wanted == j, block, rim)
    rim_coeff = jnp.where(is_low, conductivity_terms[0], conductivity_terms[-1])
    rim = jnp.concatenate([rim.reshape(2 * modes, cells), rim_coeff], 0)
    route = []
    for s in range(n_space):
        for t in range(n_term):
            low, high = s * n_term + t, (s + 1) % n_space * n_term + t
            route.append((high, low) if t < n_term // 2 else (low, high))
    halo = lax.ppermute(rim, ("space", "term"), route)

    for stage in range(half, pairs - 1):
        value = go(stage, value, halo)
    arguments = (n_term, n_space, conductivity_terms, blocks, halo, value)
    keep, send = run_last(False, *arguments)
    leaving = keep + exchange(send, "space", 1)
    away = exchange(leaving, "space", 2)
    value = after(value, leaving)
    keep, send = run_last(True, n_term, n_space, conductivity_terms, blocks, halo, value)
    middle = terms // 2
    came = [exchange(send[:, :middle], "space", 1), exchange(send[:, middle:], "space", 1)]
    total = keep + jnp.concatenate(came, 1) + away
    apart = 4
    while apart < n_space:
        bit = space_at // apart % 2
        halves = total.reshape((total.shape[0] // 2, 2) + total.shape[1:])
        send = lax.dynamic_index_in_dim(halves, 1 - bit, 1, keepdims=False)
        keep = lax.dynamic_index_in_dim(halves, bit, 1, keepdims=False)
        total = keep + exchange(send, "space", apart)
        apart *= 2
    return total[0]


def solution(mesh):
    placed = (
        P(("space", "term"), None, None),
        P(("space", "term"), None, None),
        P("space", "term", None),
    )
    return jax.shard_map(
        local, mesh=mesh, in_specs=placed, out_specs=P("term", "space"), check_vma=False
    )
```
